512 devices in a mesh: prompt: 4 (over y_hi), sample: 16 (over y_lo, x, core), tensor: 8 (over z).
Axes of the slice: x: 4, y: 8 (y_hi: 4, y_lo: 2; y = y_hi * 2 + y_lo), z: 8, core: 2. Of those that a mesh axis runs over, the one named last changes fastest.
Arguments:
- hidden_in: float32 [1536, 5120], P('prompt', 'sample'), parts along dimension 0, may hold values from -12 to 12
- prompt_len: int32 [16], P('prompt'), parts along dimension 0, may hold values from 1 to 1024, 2048 in all
- cached_prompt_keys: bfloat16 [2, 8192, 8, 128], P(None, ('prompt', 'sample'), 'tensor'), parts along dimension 1, may hold values from -900 to 900
- cached_prompt_values: bfloat16 [2, 8192, 8, 128], P(None, ('prompt', 'sample'), 'tensor'), parts along dimension 1, may hold values from -6 to 6
- query_key_value_weight: bfloat16 [2, 5120, 10240], P(None, 'sample', 'tensor'), may hold values from -1 to 1
- w_out: bfloat16 [2, 8192, 5120], P(None, 'tensor', 'sample'), may hold values from -0.0625 to 0.0625
Outputs:
- hidden_out: float32 [1536, 5120], P('prompt', 'sample'), parts along dimension 0
The draws below stay inside these ranges and needn't reach their ends.
There are 4 independent parts, one for each index of `prompt`. The reference program is written for one: setup_inputs(seed, part) draws one part's arguments, and reference() takes and returns one part's arrays. A program takes and returns all parts, laid end to end along the dimension named above; an argument that names none is the same for every part. Nothing has to cross between parts.
Inputs may be any that keep to these rules, and one draw needn't show every extreme that they name: `prompt_len`: the lengths sum to 2048, and one of them is exactly 1024.
All inputs are finite; a program needn't handle non-finite values.
Results may differ from the reference program's by a relative error of at most 0.0065.
Values may be sent and summed in bfloat16 or wider, within the bound.
A program may use at most 64 MiB of HBM per device.

```python
import math
import jax
import jax.numpy as jnp
import numpy as np
from jax import lax

MODEL_WIDTH = 5120
QUERY_HEADS = 64
KEY_VALUE_HEADS = 8
HEAD_SIZE = 128
LAYER_TOTAL = 2
STEPS = 6
NPR = 4
SAMPLE_PROMPT = 128
PROMPT_SLOTS = 2048
ROWS = 384
N_SAMPLE = 16


def draw_cached_prompt_keys(key, part):
    key = jax.random.fold_in(key, 11)
    sampled_keys = jax.random.truncated_normal(key, -6.0, 6.0, (LAYER_TOTAL, PROMPT_SLOTS, KEY_VALUE_HEADS, HEAD_SIZE), jnp.float32)
    return sampled_keys.astype(jnp.bfloat16)


def draw_hidden_in(key, part):
    key = jax.random.fold_in(key, 23)
    place = jnp.arange(MODEL_WIDTH, dtype=jnp.float32) / (MODEL_WIDTH - 1)
    entries = jax.random.truncated_normal(key, -6.0, 6.0, (ROWS, MODEL_WIDTH), jnp.float32)
    column_scale = 0.5 * 4.0 ** place
    values_out = entries * column_scale[None, :]
    return jnp.clip(values_out, -12.0, 12.0)


def draw_query_key_value_weight(key, part):
    key = jax.random.fold_in(key, 37)
    group_cols = (QUERY_HEADS // KEY_VALUE_HEADS + 2) * HEAD_SIZE
    columns = KEY_VALUE_HEADS * group_cols
    entries = jax.random.truncated_normal(key, -6.0, 6.0, (LAYER_TOTAL, MODEL_WIDTH, columns), jnp.float32)
    column_ids = jnp.arange(columns, dtype=jnp.int32)
    is_query = column_ids % group_cols < QUERY_HEADS // KEY_VALUE_HEADS * HEAD_SIZE
    column_scale = jnp.where(is_query, 3.0, 1.0)
    return jnp.clip(entries * column_scale[None, None, :] * MODEL_WIDTH ** (-0.5), -1.0, 1.0).astype(jnp.bfloat16)


def shard_levels(key, shape, pieces, smallest, top_value):
    loudness = 1.0
    for axis_at, parts in pieces:
        steps = jax.random.uniform(jax.random.fold_in(jax.random.fold_in(key, 6), axis_at), (parts,), jnp.float32, smallest / len(pieces), top_value / len(pieces))
        loudness = loudness * jnp.repeat(jnp.exp(steps), shape[axis_at] // parts).reshape((-1,) + (1,) * (len(shape) - 1 - axis_at))
    return loudness


def profile(number_of, total, limit, slope):
    weights = [(1 << 20) // math.isqrt(rank ** slope) + 1 for rank in range(2, number_of + 1)]
    spare, counts = total - limit - (number_of - 1), [1] * (number_of - 1)
    while spare > 0:
        free = [i for i in range(number_of - 1) if counts[i] < limit]
        pool, budget = sum([weights[i] for i in free]), spare
        for i in free:
            addition = min(limit - counts[i], max(1, budget * weights[i] // pool), spare)
            counts[i] = counts[i] + addition
            spare = spare - addition
    return np.array([limit] + counts)


def uneven(key, number_of, total, most, lean):
    if number_of == 2:
        one = jax.random.randint(key, (), max(1, total - most), min(most, total - 1) + 1)
        return jnp.stack([one, total - one])
    sizes = jnp.asarray(profile(number_of, total, most, lean), jnp.int32)
    pairs = (number_of - 1) // 2
    source_of, taker = sizes[1:1 + 2 * pairs:2], sizes[2:2 + 2 * pairs:2]
    slack = jnp.minimum(source_of - 1, most - taker)
    moved = jax.random.randint(jax.random.fold_in(key, 1), (pairs,), 0, 1 << 20) % (slack + 1)
    sizes = sizes.at[1:1 + 2 * pairs:2].set(source_of - moved).at[2:2 + 2 * pairs:2].set(taker + moved)
    return sizes[jax.random.permutation(jax.random.fold_in(key, 2), number_of)]


def gaussian(key, dims, deviation, bound, pieces=(), kind=jnp.bfloat16):
    values = jax.random.normal(key, dims, jnp.float32) * deviation
    if len(pieces) > 0:
        values = shard_levels(key, dims, pieces, -0.22, 0.18) * values
    return jnp.clip(values, min=-bound, max=bound).astype(kind)


def setup_inputs(seed: int = 0, part: int = 0) -> dict:
    key_list = jax.random.split(jax.random.key(seed), 7)
    part_keys = jax.random.split(jax.random.fold_in(key_list[6], part), 7)
    return {
        "hidden_in": draw_hidden_in(jax.random.fold_in(jax.random.fold_in(key_list[6], part), 71), part),
        "prompt_len": uneven(part_keys[1], NPR, PROMPT_SLOTS, PROMPT_SLOTS // 2, 2).astype(jnp.int32),
        "cached_prompt_keys": draw_cached_prompt_keys(jax.random.fold_in(jax.random.fold_in(key_list[6], part), 71), part),
        "cached_prompt_values": gaussian(part_keys[3], (LAYER_TOTAL, PROMPT_SLOTS, KEY_VALUE_HEADS, HEAD_SIZE), 1.0, 6.0, ((1, 16), (2, 8))),
        "query_key_value_weight": draw_query_key_value_weight(jax.random.fold_in(key_list[6], 71), part),
        "w_out": gaussian(key_list[5], (LAYER_TOTAL, QUERY_HEADS * HEAD_SIZE, MODEL_WIDTH), (QUERY_HEADS * HEAD_SIZE) ** -0.5, 0.0625, ((1, 8), (2, 16))),
    }


rope_base = 1000000.0
epsilon = 1e-06
score_after_mask = -1e+30

def rotate(vector, positions):
    half_dim = vector.shape[-1] // 2
    frequency = rope_base ** (-2.0 * jnp.arange(half_dim, dtype=jnp.float32) / vector.shape[-1])
    target_shape = (positions.shape[0],) + (1,) * (vector.ndim - 2) + (half_dim,)
    angles = (positions[:, None] * frequency[None, :]).reshape(target_shape)
    cosine = jnp.cos(angles)
    sine_part = jnp.sin(angles)
    leading = vector[..., :half_dim]
    trailing = vector[..., half_dim:]
    return jnp.concatenate([leading * cosine - trailing * sine_part, trailing * cosine + leading * sine_part], axis=-1)

def softmax_parts(scores, visible):
    scores = jnp.where(visible, scores, score_after_mask)
    maxima = lax.optimization_barrier(jnp.max(scores, axis=-1))
    weights = jnp.where(visible, jnp.exp(scores - maxima[..., None]), 0.0)
    totals = lax.optimization_barrier(jnp.sum(weights, axis=-1))
    rounded = lax.optimization_barrier(weights.astype(jnp.bfloat16)).astype(jnp.float32)
    return (maxima, rounded, totals)

def block_stats(queries, keys, values, visible):
    scale_factor = keys.shape[-1] ** (-0.5)
    scores = jnp.einsum('rgqd,ngd->rgqn', queries.astype(jnp.float32), keys.astype(jnp.float32), precision=lax.Precision.HIGHEST) * scale_factor
    maxima, rounded, totals = softmax_parts(scores, visible[:, None, None, :])
    partial_value = jnp.einsum('rgqn,ngd->rgqd', rounded, values.astype(jnp.float32), precision=lax.Precision.HIGHEST)
    return (maxima, partial_value, totals)

def recent_stats(queries, new_keys, new_values):
    number_of_rows, kv_heads, queries_per_group, head_dim = queries.shape
    samples_here = number_of_rows // STEPS
    query_view = queries.reshape(samples_here, STEPS, kv_heads, queries_per_group, head_dim).astype(jnp.float32)
    key_view = new_keys.reshape(samples_here, STEPS, kv_heads, head_dim).astype(jnp.float32)
    value_view = new_values.reshape(samples_here, STEPS, kv_heads, head_dim).astype(jnp.float32)
    scores = jnp.einsum('stgqd,sugd->stgqu', query_view, key_view, precision=lax.Precision.HIGHEST) * head_dim ** (-0.5)
    steps_here = jnp.arange(STEPS, dtype=jnp.int32)
    visible = (steps_here[None, :] <= steps_here[:, None])[None, :, None, None, :]
    maxima, rounded, totals = softmax_parts(scores, visible)
    partial_value = jnp.einsum('stgqu,sugd->stgqd', rounded, value_view, precision=lax.Precision.HIGHEST)
    return (maxima.reshape(number_of_rows, kv_heads, queries_per_group), partial_value.reshape(number_of_rows, kv_heads, queries_per_group, head_dim), totals.reshape(number_of_rows, kv_heads, queries_per_group))

def combine(earlier, later):
    peak = jnp.maximum(earlier[0], later[0])
    scale_left = jnp.exp(earlier[0] - peak)
    scale_right = jnp.exp(later[0] - peak)
    return (peak, earlier[1] * scale_left[..., None] + later[1] * scale_right[..., None], earlier[2] * scale_left + later[2] * scale_right)

def reference(hidden_in, prompt_len, cached_prompt_keys, cached_prompt_values, query_key_value_weight, w_out):
    number_of_rows = hidden_in.shape[0]
    queries_per_group = QUERY_HEADS // KEY_VALUE_HEADS
    row_ids = jnp.arange(number_of_rows, dtype=jnp.int32)
    prompt_of = row_ids // STEPS % NPR
    offsets = (jnp.cumsum(prompt_len) - prompt_len).astype(jnp.int32)
    row_len = prompt_len[prompt_of].astype(jnp.int32)
    row_start = offsets[prompt_of]
    row_end = row_start + row_len
    positions = (row_len + row_ids % STEPS).astype(jnp.float32)
    stream = hidden_in
    for layer_position in range(LAYER_TOTAL):
        inverse_root_mean = lax.rsqrt(lax.optimization_barrier(jnp.sum(stream * stream, axis=1)) / MODEL_WIDTH + epsilon)
        stream_half = stream.astype(jnp.bfloat16)
        reduced_total = jnp.dot(stream_half, query_key_value_weight[layer_position], preferred_element_type=jnp.float32)
        weighted_values = (reduced_total * inverse_root_mean[:, None]).reshape(number_of_rows, KEY_VALUE_HEADS, queries_per_group + 2, HEAD_SIZE)
        queries = rotate(weighted_values[:, :, :queries_per_group, :], positions)
        new_keys = rotate(weighted_values[:, :, queries_per_group, :], positions).astype(jnp.bfloat16)
        new_values = weighted_values[:, :, queries_per_group + 1, :].astype(jnp.bfloat16)
        key_block_grid = cached_prompt_keys[layer_position].reshape(N_SAMPLE, SAMPLE_PROMPT, KEY_VALUE_HEADS, HEAD_SIZE)
        value_block_grid = cached_prompt_values[layer_position].reshape(N_SAMPLE, SAMPLE_PROMPT, KEY_VALUE_HEADS, HEAD_SIZE)

        def visit(running, items):
            keys_here, values_here, block_number = items
            key_pos = block_number * SAMPLE_PROMPT + jnp.arange(SAMPLE_PROMPT, dtype=jnp.int32)
            visible = (key_pos[None, :] >= row_start[:, None]) & (key_pos[None, :] < row_end[:, None])
            return (combine(running, block_stats(queries, keys_here, values_here, visible)), None)
        starting_value = (jnp.full((number_of_rows, KEY_VALUE_HEADS, queries_per_group), score_after_mask, jnp.float32), jnp.zeros((number_of_rows, KEY_VALUE_HEADS, queries_per_group, HEAD_SIZE), jnp.float32), jnp.zeros((number_of_rows, KEY_VALUE_HEADS, queries_per_group), jnp.float32))
        summary, ignored = lax.scan(visit, starting_value, (key_block_grid, value_block_grid, jnp.arange(N_SAMPLE, dtype=jnp.int32)))
        summary = combine(summary, recent_stats(queries, new_keys, new_values))
        attention = (summary[1] / summary[2][..., None]).astype(jnp.bfloat16).reshape(number_of_rows, QUERY_HEADS * HEAD_SIZE)
        update = jnp.dot(attention, w_out[layer_position], preferred_element_type=jnp.float32)
        stream = stream + update
    return stream
```

```python
import jax
import jax.numpy as jnp
import numpy as np
from jax import lax
from jax.experimental import pallas as pl
from jax.experimental.pallas import tpu as pltpu
from jax.sharding import PartitionSpec as P

STEPS = 6
NPR = 4
HEADS = 8
HEAD = 128
LAYERS = 2
ROPE_BASE = 1000000.0
EPSILON = 1e-06
NEGATIVE = -1e30
WIDTH = 5120
ROWS = 384
OWN = 24
CHIP = 48
COLS = 320
PAD = 384
PART0 = 640
PART1 = 640
WIDE0 = PART0 + 128
PACKED = 120
COPIES = 128
MESH = pl.DeviceIdType.MESH
F32 = jnp.float32
BF16 = jnp.bfloat16


def dot(a, b):
    return jnp.dot(a, b, preferred_element_type=F32)


def dot_across(a, b):
    return lax.dot_general(a, b, (((1,), (1,)), ((), ())), preferred_element_type=F32)


def iota(shape, axis):
    return lax.broadcasted_iota(jnp.int32, shape, axis)


def pack(block):
    tail = block[:, 256:384]
    low = iota((OWN, 128), 1) < 64
    both = jnp.where(low, tail[:OWN], pltpu.roll(tail[OWN:], 64, 1))
    return jnp.concatenate([block[:, 0:128], block[:, 128:256], both], axis=0)


def unpack_tail(packed):
    both = packed[2 * CHIP :]
    return jnp.concatenate([both, pltpu.roll(both, 64, 1)], axis=0)


def kernel(
    len_ref, freq_ref, hid_hbm, key_hbm, val_hbm, win_hbm, wout_hbm, out_ref,
    hid_across, hid, win, wpad, kv, hs, c0s, c1s, c0r, c1r, s0, s1,
    x0relay, x0dir, x0fin, x1relay, x1dir, x1fin, y1r, y0r,
    q3, low_ref, high_ref, cos_ref, sin_ref, gat, ob, d1r, d2r, sg, fg, str1, out_rows,
    load_sem, send_sem, recv_sem,
):
    s = lax.axis_index("sample")
    z = lax.axis_index("tensor")
    core = s % 2
    chip = s // 2
    x = chip % 4
    y = chip // 4
    other = 1 - y
    sigma = 1 - 2 * core
    ahead = (x + sigma + 4) % 4
    behind = (x - sigma + 4) % 4
    far = (x + 2) % 4
    delta = 2 * ((z + core) % 2) - 1

    def place(py, px, pc):
        return (py * 4 + px) * 2 + pc

    def ring(step):
        return (z + delta * step + 8) % 8

    sibling = {"sample": place(y, x, 1 - core)}
    to_ahead = {"sample": place(y, ahead, core)}
    to_behind = {"sample": place(y, behind, core)}
    to_other = {"sample": place(other, x, core)}
    partner = {"tensor": ring(-1)}

    used = [0]
    pending = []

    def ids(count):
        first = used[0]
        used[0] += count
        return first

    def send(index, src, dst, device):
        copy = pltpu.make_async_remote_copy(
            src_ref=src, dst_ref=dst, send_sem=send_sem.at[index], recv_sem=recv_sem.at[index],
            device_id=device, device_id_type=MESH,
        )
        copy.start()
        pending.append(copy)

    def arrived(index, ref):
        pltpu.make_async_remote_copy(
            src_ref=ref, dst_ref=ref, send_sem=send_sem.at[index], recv_sem=recv_sem.at[index],
            device_id=sibling, device_id_type=MESH,
        ).wait_recv()

    def drain():
        for copy in pending:
            copy.wait_send()
        pending.clear()

    loads = {}

    def load(name, index, src, dst):
        loads[name] = pltpu.make_async_copy(src, dst, load_sem.at[index])
        loads[name].start()

    load("hid", 0, hid_hbm, hid_across.at[pl.ds(0, COLS)])
    load("win0", 1, win_hbm.at[0], win.at[0])
    for layer in range(LAYERS):
        load(("key", layer), 2 + 2 * layer, key_hbm.at[layer], kv.at[layer, s, 0])
        load(("val", layer), 3 + 2 * layer, val_hbm.at[layer], kv.at[layer, s, 1])
    load(("wout", 0), 6, wout_hbm.at[0], wpad.at[0, pl.ds(0, COLS)])
    load("win1", 7, win_hbm.at[1], win.at[1])
    load(("wout", 1), 8, wout_hbm.at[1], wpad.at[1, pl.ds(0, COLS)])
    hid_across[COLS:] = jnp.zeros((PAD - COLS, ROWS), F32)
    for layer in range(LAYERS):
        wpad[layer, COLS:] = jnp.zeros((PAD - COLS, 1024), BF16)

    barrier = pltpu.get_barrier_semaphore()
    near = [sibling, to_ahead, to_behind, to_other]
    near += [{"tensor": ring(step)} for step in (-1, 1, 2, -2, 3)]
    for device in near:
        pl.semaphore_signal(barrier, inc=1, device_id=device, device_id_type=MESH)
    pl.semaphore_wait(barrier, len(near))

    class Gather:
        def __init__(self, buf):
            self.buf = buf
            self.first = ids(15)

        def put(self, number, py, px, device, pc=None):
            block = self.buf.at[place(py, px, core)]
            send(self.first + number, block, block, device)

        def get(self, number, py, px, pc=None):
            where = place(py, px, core if pc is None else pc)
            arrived(self.first + number, self.buf.at[where])

        def begin(self):
            self.put(0, y, x, to_other)
            self.put(1, y, x, to_ahead)
            self.put(2, y, x, to_behind)
            self.put(7, y, x, sibling)

        def cross(self):
            self.get(0, other, x)
            self.put(4, other, x, to_ahead)
            self.put(5, other, x, to_behind)
            self.put(11, other, x, sibling)

        def along(self, half):
            py, at, near_core = (y, 1, 8) if half == 0 else (other, 4, 12)
            self.get(at, py, behind)
            self.put(at + 2, py, behind, to_ahead)
            self.put(near_core, py, behind, sibling)
            self.get(at + 1, py, ahead)
            self.put(near_core + 1, py, ahead, sibling)

        def last(self, half):
            py, at, near_core = (y, 3, 10) if half == 0 else (other, 6, 14)
            self.get(at, py, far)
            self.put(near_core, py, far, sibling)

        def core_side(self, half):
            py, at = (y, 7) if half == 0 else (other, 11)
            for number, px in enumerate((x, ahead, behind, far)):
                self.get(at + number, py, px, 1 - core)

    gathers = [Gather(kv.at[layer]) for layer in range(LAYERS)]
    loads[("key", 0)].wait()
    loads[("val", 0)].wait()
    gathers[0].begin()

    loads["hid"].wait()
    hid[...] = hid_across[...].T
    for parity in range(2):
        pieces = [hid[CHIP * q + OWN * parity : CHIP * q + OWN * parity + OWN, :COLS] for q in range(8)]
        hs[parity] = jnp.concatenate(pieces, axis=0).astype(BF16)
        for q in range(8):
            squares = jnp.sum(pieces[q] * pieces[q], axis=1, keepdims=True)
            target = s0.at[q % 4, q // 4] if parity == 0 else c0s.at[q % 4, q // 4]
            target[:, PART0:] = jnp.broadcast_to(squares, (OWN, 128))
    flip = core == 1
    for q in range(8):
        zero_rows = s0[q % 4, q // 4, :, PART0:]
        one_rows = c0s[q % 4, q // 4, :, PART0:]
        s0[q % 4, q // 4, :, PART0:] = jnp.where(flip, one_rows, zero_rows)
        c0s[q % 4, q // 4, :, PART0:] = jnp.where(flip, zero_rows, one_rows)
    loads["win0"].wait()

    def tables():
        row = iota((OWN, 128), 0)
        lane = iota((OWN, 128), 1)
        prompt = lax.shift_right_logical(row * 43, 8)
        step = row - prompt * STEPS
        length = jnp.zeros((OWN, 128), jnp.int32)
        start = jnp.zeros((OWN, 128), jnp.int32)
        offset = jnp.int32(0)
        for k in range(NPR):
            length = jnp.where(prompt == k, len_ref[k], length)
            start = jnp.where(prompt == k, offset, start)
            offset = offset + len_ref[k]
        low_ref[...] = start - lane
        high_ref[...] = start + length - lane
        angle = (length + step).astype(F32) * freq_ref[...]
        cos_ref[...] = jnp.cos(angle)
        sin_ref[...] = jnp.where(lane < 64, -jnp.sin(angle), jnp.sin(angle))

    def project(layer):
        first = ids(14)
        sib = hs[1 - core]
        weights = win.at[layer]
        part = dot(sib, weights[:, PART0:])
        c1s[...] = part.reshape(2, 4, OWN, PART1)
        send(first + 0, c1s.at[other], c1r.at[layer, other], sibling)
        part = dot(sib, weights[:, :PART0])
        for q in range(8):
            c0s[q % 4, q // 4, :, :PART0] = part[OWN * q : OWN * q + OWN]
        send(first + 1, c0s.at[far], c0r.at[layer, far], sibling)
        send(first + 2, c0s.at[ahead], c0r.at[layer, ahead], sibling)
        send(first + 3, c0s.at[behind], c0r.at[layer, behind], sibling)
        send(first + 4, c0s.at[x], c0r.at[layer, x], sibling)
        send(first + 5, c1s.at[y], c1r.at[layer, y], sibling)
        mine = hs[core]
        part = dot(mine, weights[:, PART0:])
        s1[...] = part.reshape(2, 4, OWN, PART1)
        part = dot(mine, weights[:, :PART0])
        for q in range(8):
            s0[q % 4, q // 4, :, :PART0] = part[OWN * q : OWN * q + OWN]

        def core_sum(index, total, came):
            arrived(index, came)
            total[...] = total[...] + came[...]

        core_sum(first + 0, s1.at[other], c1r.at[layer, other])
        send(first + 6, s1.at[other], y1r.at[layer], to_other)
        core_sum(first + 1, s0.at[far], c0r.at[layer, far])
        send(first + 7, s0.at[far], x0relay.at[layer], to_ahead)
        core_sum(first + 2, s0.at[behind], c0r.at[layer, behind])
        send(first + 8, s0.at[behind], x0dir.at[layer], to_behind)
        core_sum(first + 3, s0.at[ahead], c0r.at[layer, ahead])
        core_sum(first + 4, s0.at[x], c0r.at[layer, x])
        core_sum(first + 5, s1.at[y], c1r.at[layer, y])
        if layer == 0:
            gathers[0].cross()
            gathers[0].along(0)
            tables()
        arrived(first + 7, x0relay.at[layer])
        s0[ahead] = s0[ahead] + x0relay[layer]
        send(first + 9, s0.at[ahead], x0fin.at[layer], to_ahead)
        arrived(first + 6, y1r.at[layer])
        s1[y] = s1[y] + y1r[layer]
        send(first + 10, s1.at[y, far], x1relay.at[layer], to_ahead)
        send(first + 11, s1.at[y, behind], x1dir.at[layer], to_behind)
        if layer == 0:
            gathers[0].last(0)
            gathers[0].along(1)
        arrived(first + 10, x1relay.at[layer])
        s1[y, ahead] = s1[y, ahead] + x1relay[layer]
        send(first + 12, s1.at[y, ahead], x1fin.at[layer], to_ahead)
        arrived(first + 8, x0dir.at[layer])
        arrived(first + 9, x0fin.at[layer])
        s0[x] = s0[x] + x0dir[layer] + x0fin[layer]
        send(first + 13, s0.at[x, other], y0r.at[layer], to_other)
        if layer == 0:
            gathers[0].last(1)
            gathers[0].core_side(0)
            gathers[0].core_side(1)
        arrived(first + 11, x1dir.at[layer])
        arrived(first + 12, x1fin.at[layer])
        part1 = s1[y, x] + x1dir[layer] + x1fin[layer]
        arrived(first + 13, y0r.at[layer])
        part0 = s0[x, y] + y0r[layer]
        return part0, part1

    def attend(layer, part0, part1):
        inverse = lax.rsqrt(part0[:, PART0:] / WIDTH + EPSILON)
        cosine = cos_ref[...]
        sine = sin_ref[...]

        def rotate(vector):
            return vector * cosine + pltpu.roll(vector, 64, 1) * sine

        blocks = [part0[:, HEAD * h : HEAD * h + HEAD] * inverse for h in range(5)]
        blocks += [part1[:, HEAD * h : HEAD * h + HEAD] * inverse for h in range(5)]
        queries = jnp.concatenate([rotate(block) for block in blocks[:HEADS]], axis=0)
        rows = HEADS * OWN
        first = queries.astype(BF16)
        rest = queries - first.astype(F32)
        second = rest.astype(BF16)
        third = (rest - second.astype(F32)).astype(BF16)
        q3[0:rows] = first
        q3[rows : 2 * rows] = second
        q3[2 * rows :] = third
        empty = jnp.zeros((128 - OWN, HEAD), F32)
        kv[layer, 16, 0] = jnp.concatenate([rotate(blocks[8]), empty], axis=0).astype(BF16)
        kv[layer, 16, 1] = jnp.concatenate([blocks[9], empty], axis=0).astype(BF16)

        def visit(block, seen, running):
            peak, total, summed = running
            scores = dot_across(q3[...], kv[layer, block, 0])
            scores = (scores[2 * rows :] + scores[rows : 2 * rows]) + scores[:rows]
            bias = jnp.where(seen, 0.0, NEGATIVE)
            factor = jnp.where(seen, 1.0, 0.0)
            scores = (scores * HEAD**-0.5).reshape(HEADS, OWN, 128) + bias[None]
            maxima = jnp.max(scores, axis=-1, keepdims=True)
            weights = jnp.exp(scores - maxima) * factor[None]
            sums = jnp.sum(weights, axis=-1, keepdims=True)
            values = dot(weights.reshape(rows, 128).astype(BF16), kv[layer, block, 1])
            higher = jnp.maximum(peak, maxima)
            left = jnp.exp(peak - higher)
            right = jnp.exp(maxima - higher)
            return (
                higher,
                total * left + sums * right,
                summed * left + values.reshape(HEADS, OWN, HEAD) * right,
            )

        def prompt_block(block, running):
            at = block * 128
            seen = (low_ref[...] <= at) & (high_ref[...] > at)
            return visit(block, seen, running)

        running = (
            jnp.full((HEADS, OWN, 1), NEGATIVE, F32),
            jnp.zeros((HEADS, OWN, 1), F32),
            jnp.zeros((HEADS, OWN, HEAD), F32),
        )
        running = lax.fori_loop(0, 16, prompt_block, running, unroll=2)
        row = iota((OWN, 128), 0)
        lane = iota((OWN, 128), 1)
        row_sample = lax.shift_right_logical(row * 43, 8)
        lane_sample = lax.shift_right_logical(lane * 43, 8)
        recent = (row_sample == lane_sample) & (lane <= row)
        _, total, summed = visit(16, recent, running)
        attention = summed / total
        top = jnp.concatenate([attention[h] for h in range(4)], axis=1)
        bottom = jnp.concatenate([attention[h] for h in range(4, 8)], axis=1)
        gat[layer, s] = jnp.concatenate([top, bottom], axis=0).astype(BF16)

    def collect(layer):
        gather = Gather(gat.at[layer])
        gather.begin()
        gather.cross()
        gather.along(0)
        gather.along(1)
        gather.last(0)
        gather.last(1)

        def product(half):
            rows = gat[layer, pl.ds(half * 8, 8)].reshape(8 * CHIP, 512)
            upper = dot_across(rows, wpad[layer, :, :512])
            lower = dot_across(rows, wpad[layer, :, 512:])
            for q in range(4):
                at = 2 * CHIP * q
                block = jnp.concatenate(
                    [
                        upper[at : at + OWN] + lower[at + OWN : at + CHIP],
                        upper[at + CHIP : at + CHIP + OWN] + lower[at + CHIP + OWN : at + 2 * CHIP],
                    ],
                    axis=0,
                )
                ob[half * 4 + q] = pack(block)

        loads[("wout", layer)].wait()
        gather.core_side(0)
        product(y)
        gather.core_side(1)
        product(other)

    def tensor_sum(layer):
        first = ids(7)
        for k in (3, 2, 1, 0):
            send(first + k, ob.at[ring(-1 - k)], d1r.at[layer, k], partner)
        if layer == 0:
            loads[("key", 1)].wait()
            loads[("val", 1)].wait()
            gathers[1].begin()
        for k in (3, 2, 1):
            at = ring(k)
            arrived(first + k, d1r.at[layer, k])
            ob[at] = ob[at] + d1r[layer, k]
            send(first + 3 + k, ob.at[at], d2r.at[layer, k - 1], {"tensor": at})
        arrived(first + 0, d1r.at[layer, 0])
        total = ob[z] + d1r[layer, 0]
        if layer == 0:
            gathers[1].cross()
            gathers[1].along(0)
        for k in (1, 2, 3):
            arrived(first + 3 + k, d2r.at[layer, k - 1])
            total = total + d2r[layer, k - 1]
        return total

    def tensor_gather(buf):
        first = ids(7)
        mine = buf.at[z]
        send(first + 2, mine, mine, {"tensor": ring(3)})
        send(first + 1, mine, mine, {"tensor": ring(-2)})
        send(first + 0, mine, mine, {"tensor": ring(1)})
        send(first + 3, mine, mine, partner)
        for k in (1, 2, 3):
            block = buf.at[ring(k)]
            arrived(first + k - 1, block)
            send(first + 3 + k, block, block, partner)
        for k in (0, 1, 2, 3):
            arrived(first + 3 + k, buf.at[ring(-1 - k)])

    part0, part1 = project(0)
    attend(0, part0, part1)
    collect(0)
    stream = pack(hid[pl.ds(pl.multiple_of(z * CHIP, 8), CHIP), :]) + tensor_sum(0)
    str1[...] = stream
    tail = unpack_tail(stream)
    lane = iota((CHIP, 128), 1)
    middle0 = stream[:CHIP]
    middle1 = stream[CHIP : 2 * CHIP]
    kept = jnp.where(lane < 64, tail, 0.0)
    squares = jnp.sum(middle0 * middle0 + middle1 * middle1 + kept * kept, axis=1, keepdims=True)
    square1 = squares.astype(BF16).astype(F32)
    square2 = (squares - square1).astype(BF16).astype(F32)
    square3 = squares - square1 - square2
    kept = jnp.where(lane == 64, square1, kept)
    kept = jnp.where(lane == 65, square2, kept)
    kept = jnp.where(lane == 66, square3, kept)
    sg[z] = jnp.concatenate([middle0, middle1, kept], axis=1).astype(BF16)
    tensor_gather(sg)
    gathers[1].last(0)
    gathers[1].along(1)
    drain()

    flip = core == 1
    by_parity = [[], []]
    for q in range(8):
        block = sg[q].astype(F32)
        sums = jnp.sum(jnp.where(lane >= 64, block[:, 256:], 0.0), axis=1, keepdims=True)
        sums = jnp.broadcast_to(sums, (CHIP, 128))
        s0[q % 4, q // 4, :, PART0:] = jnp.where(flip, sums[OWN:], sums[:OWN])
        c0s[q % 4, q // 4, :, PART0:] = jnp.where(flip, sums[:OWN], sums[OWN:])
        for parity in range(2):
            by_parity[parity].append(block[OWN * parity : OWN * parity + OWN, :COLS])
    for parity in range(2):
        hs[parity] = jnp.concatenate(by_parity[parity], axis=0).astype(BF16)
    loads["win1"].wait()
    part0, part1 = project(1)
    gathers[1].last(1)
    gathers[1].core_side(0)
    gathers[1].core_side(1)
    attend(1, part0, part1)
    collect(1)
    fg[z] = str1[...] + tensor_sum(1)
    tensor_gather(fg)
    for d in range(8):
        block = fg[d]
        rows = slice(CHIP * d, CHIP * d + CHIP)
        out_rows[rows, 0:128] = block[:CHIP]
        out_rows[rows, 128:256] = block[CHIP : 2 * CHIP]
        out_rows[rows, 256:384] = unpack_tail(block)
    out_ref[...] = out_rows[...].T[:COLS]
    drain()


def on_device(hidden_in, prompt_len, cached_prompt_keys, cached_prompt_values, query_key_value_weight, w_out):
    keys = cached_prompt_keys.reshape(LAYERS, 128, HEAD)
    values = cached_prompt_values.reshape(LAYERS, 128, HEAD)
    half = np.power(ROPE_BASE, -2.0 * np.arange(64) / HEAD)
    freq = jnp.asarray(np.concatenate([half, half])[None, :], F32)
    vmem = pltpu.VMEM
    scratch = [
        vmem((PAD, ROWS), F32),
        vmem((ROWS, PAD), F32),
        vmem((LAYERS, COLS, 1280), BF16),
        vmem((LAYERS, PAD, 1024), BF16),
        vmem((LAYERS, 17, 2, 128, HEAD), BF16),
        vmem((2, 192, COLS), BF16),
        vmem((4, 2, OWN, WIDE0), F32),
        vmem((2, 4, OWN, PART1), F32),
        vmem((LAYERS, 4, 2, OWN, WIDE0), F32),
        vmem((LAYERS, 2, 4, OWN, PART1), F32),
        vmem((4, 2, OWN, WIDE0), F32),
        vmem((2, 4, OWN, PART1), F32),
        vmem((LAYERS, 2, OWN, WIDE0), F32),
        vmem((LAYERS, 2, OWN, WIDE0), F32),
        vmem((LAYERS, 2, OWN, WIDE0), F32),
        vmem((LAYERS, OWN, PART1), F32),
        vmem((LAYERS, OWN, PART1), F32),
        vmem((LAYERS, OWN, PART1), F32),
        vmem((LAYERS, 4, OWN, PART1), F32),
        vmem((LAYERS, OWN, WIDE0), F32),
        vmem((3 * HEADS * OWN, HEAD), BF16),
        vmem((OWN, 128), jnp.int32),
        vmem((OWN, 128), jnp.int32),
        vmem((OWN, 128), F32),
        vmem((OWN, 128), F32),
        vmem((LAYERS, 16, CHIP, 512), BF16),
        vmem((8, PACKED, 128), F32),
        vmem((LAYERS, 4, PACKED, 128), F32),
        vmem((LAYERS, 3, PACKED, 128), F32),
        vmem((8, CHIP, PAD), BF16),
        vmem((8, PACKED, 128), F32),
        vmem((PACKED, 128), F32),
        vmem((ROWS, PAD), F32),
        pltpu.SemaphoreType.DMA((9,)),
        pltpu.SemaphoreType.DMA((COPIES,)),
        pltpu.SemaphoreType.DMA((COPIES,)),
    ]
    hbm = pl.BlockSpec(memory_space=pl.ANY)
    out = pl.pallas_call(
        kernel,
        out_shape=jax.ShapeDtypeStruct((COLS, ROWS), F32),
        in_specs=[
            pl.BlockSpec(memory_space=pltpu.SMEM),
            pl.BlockSpec(memory_space=pltpu.VMEM),
            hbm, hbm, hbm, hbm, hbm,
        ],
        out_specs=pl.BlockSpec(memory_space=pltpu.VMEM),
        scratch_shapes=scratch,
        compiler_params=pltpu.CompilerParams(
            collective_id=0, has_side_effects=True, vmem_limit_bytes=60 * 1024 * 1024
        ),
        name="two_layers",
    )(prompt_len, freq, hidden_in.T, keys, values, query_key_value_weight, w_out.transpose(0, 2, 1))
    return out.T


def solution(mesh):
    return jax.shard_map(
        on_device,
        mesh=mesh,
        in_specs=(
            P("prompt", "sample"),
            P("prompt"),
            P(None, ("prompt", "sample"), "tensor", None),
            P(None, ("prompt", "sample"), "tensor", None),
            P(None, "sample", "tensor"),
            P(None, "tensor", "sample"),
        ),
        out_specs=P("prompt", "sample"),
        check_vma=False,
    )
```

```python
import jax
import jax.numpy as jnp
import numpy as np
from jax import lax
from jax.experimental import pallas as pl
from jax.experimental.pallas import tpu as pltpu
from jax.sharding import PartitionSpec as P

STEPS = 6
NPR = 4
HEADS = 8
HEAD = 128
LAYERS = 2
ROPE_BASE = 1000000.0
EPSILON = 1e-06
NEGATIVE = -1e30
WIDTH = 5120
ROWS = 384
OWN = 24
CHIP = 48
COLS = 320
PAD = 384
PART0 = 640
PART1 = 640
WIDE0 = PART0 + 128
PACKED = 120
COPIES = 128
MESH = pl.DeviceIdType.MESH
F32 = jnp.float32
BF16 = jnp.bfloat16


def dot(a, b):
    return jnp.dot(a, b, preferred_element_type=F32)


def iota(shape, axis):
    return lax.broadcasted_iota(jnp.int32, shape, axis)


def pack(block):
    tail = block[:, 256:384]
    low = iota((OWN, 128), 1) < 64
    both = jnp.where(low, tail[:OWN], pltpu.roll(tail[OWN:], 64, 1))
    return jnp.concatenate([block[:, 0:128], block[:, 128:256], both], axis=0)


def unpack_tail(packed):
    both = packed[2 * CHIP :]
    return jnp.concatenate([both, pltpu.roll(both, 64, 1)], axis=0)


def kernel(
    len_ref, freq_ref, hid_hbm, key_hbm, val_hbm, win_hbm, wout_hbm, out_ref,
    hid_across, hid, win, wpad, wout, val, kv, hs, c0s, c1s, c0r, c1r, s0, s1,
    x0relay, x0dir, x0fin, x1relay, x1dir, x1fin, y1r, y0r,
    past_ref, length_ref, cos_ref, sin_ref, gat, ob, d1r, d2r, sg, fg, str1, out_rows,
    load_sem, send_sem, recv_sem,
):
    s = lax.axis_index("sample")
    z = lax.axis_index("tensor")
    core = s % 2
    chip = s // 2
    x = chip % 4
    y = chip // 4
    other = 1 - y
    sigma = 1 - 2 * core
    ahead = (x + sigma + 4) % 4
    behind = (x - sigma + 4) % 4
    far = (x + 2) % 4
    delta = 2 * ((z + core) % 2) - 1

    def place(py, px, pc):
        return (py * 4 + px) * 2 + pc

    def ring(step):
        return (z + delta * step + 8) % 8

    def chip_of(at):
        return (at % 2) * 4 + at // 2

    sibling = {"sample": place(y, x, 1 - core)}
    to_ahead = {"sample": place(y, ahead, core)}
    to_behind = {"sample": place(y, behind, core)}
    to_other = {"sample": place(other, x, core)}
    partner = {"tensor": ring(-1)}

    used = [0]
    pending = []

    def ids(count):
        first = used[0]
        used[0] += count
        return first

    def send(index, src, dst, device):
        copy = pltpu.make_async_remote_copy(
            src_ref=src, dst_ref=dst, send_sem=send_sem.at[index], recv_sem=recv_sem.at[index],
            device_id=device, device_id_type=MESH,
        )
        copy.start()
        pending.append(copy)

    def arrived(index, ref):
        pltpu.make_async_remote_copy(
            src_ref=ref, dst_ref=ref, send_sem=send_sem.at[index], recv_sem=recv_sem.at[index],
            device_id=sibling, device_id_type=MESH,
        ).wait_recv()

    def drain():
        for copy in pending:
            copy.wait_send()
        pending.clear()

    loads = {}

    def load(name, index, src, dst):
        loads[name] = pltpu.make_async_copy(src, dst, load_sem.at[index])
        loads[name].start()

    load("hid", 0, hid_hbm, hid_across.at[pl.ds(0, COLS)])
    load("win0", 1, win_hbm.at[0], win.at[0])
    for layer in range(LAYERS):
        load(("key", layer), 2 + 2 * layer, key_hbm.at[layer], kv.at[layer, s, 0])
        load(("val", layer), 3 + 2 * layer, val_hbm.at[layer], val.at[layer])
    load(("wout", 0), 6, wout_hbm.at[0], wpad.at[0, pl.ds(0, COLS)])
    load("win1", 7, win_hbm.at[1], win.at[1])
    load(("wout", 1), 8, wout_hbm.at[1], wpad.at[1, pl.ds(0, COLS)])
    hid_across[COLS:] = jnp.zeros((PAD - COLS, ROWS), F32)
    for layer in range(LAYERS):
        wpad[layer, COLS:] = jnp.zeros((PAD - COLS, 1024), BF16)

    barrier = pltpu.get_barrier_semaphore()
    near = [sibling, to_ahead, to_behind, to_other]
    near += [{"tensor": ring(step)} for step in (-1, 1, 2, -2, 3)]
    for device in near:
        pl.semaphore_signal(barrier, inc=1, device_id=device, device_id_type=MESH)
    pl.semaphore_wait(barrier, len(near))

    class Gather:
        def __init__(self, buf):
            self.buf = buf
            self.first = ids(15)

        def put(self, number, py, px, device, pc=None):
            block = self.buf.at[place(py, px, core)]
            send(self.first + number, block, block, device)

        def get(self, number, py, px, pc=None):
            where = place(py, px, core if pc is None else pc)
            arrived(self.first + number, self.buf.at[where])

        def begin(self):
            self.put(0, y, x, to_other)
            self.put(1, y, x, to_ahead)
            self.put(2, y, x, to_behind)
            self.put(7, y, x, sibling)

        def cross(self):
            self.get(0, other, x)
            self.put(4, other, x, to_ahead)
            self.put(5, other, x, to_behind)
            self.put(11, other, x, sibling)

        def along(self, half):
            py, at, near_core = (y, 1, 8) if half == 0 else (other, 4, 12)
            self.get(at, py, behind)
            self.put(at + 2, py, behind, to_ahead)
            self.put(near_core, py, behind, sibling)
            self.get(at + 1, py, ahead)
            self.put(near_core + 1, py, ahead, sibling)

        def last(self, half):
            py, at, near_core = (y, 3, 10) if half == 0 else (other, 6, 14)
            self.get(at, py, far)
            self.put(near_core, py, far, sibling)

        def core_side(self, half):
            py, at = (y, 7) if half == 0 else (other, 11)
            for number, px in enumerate((x, ahead, behind, far)):
                self.get(at + number, py, px, 1 - core)

    gathers = [Gather(kv.at[layer]) for layer in range(LAYERS)]

    def begin_prompt(layer):
        loads[("key", layer)].wait()
        loads[("val", layer)].wait()
        kv[layer, s, 1] = val[layer].astype(F32).T.astype(BF16)
        gathers[layer].begin()

    begin_prompt(0)

    loads["hid"].wait()
    hid[...] = hid_across[...].T
    for parity in range(2):
        pieces = [hid[CHIP * q + OWN * parity : CHIP * q + OWN * parity + OWN, :COLS] for q in range(8)]
        hs[parity] = jnp.concatenate(pieces, axis=0).astype(BF16)
        for q in range(8):
            squares = jnp.sum(pieces[q] * pieces[q], axis=1, keepdims=True)
            target = s0.at[q % 4, q // 4] if parity == 0 else c0s.at[q % 4, q // 4]
            target[:, PART0:] = jnp.broadcast_to(squares, (OWN, 128))
    flip = core == 1
    for q in range(8):
        zero_rows = s0[q % 4, q // 4, :, PART0:]
        one_rows = c0s[q % 4, q // 4, :, PART0:]
        s0[q % 4, q // 4, :, PART0:] = jnp.where(flip, one_rows, zero_rows)
        c0s[q % 4, q // 4, :, PART0:] = jnp.where(flip, zero_rows, one_rows)
    loads["win0"].wait()

    def tables():
        row = iota((OWN, 128), 0)
        lane = iota((OWN, 128), 1)
        prompt = lax.shift_right_logical(row * 43, 8)
        step = row - prompt * STEPS
        length = jnp.zeros((OWN, 128), jnp.int32)
        for k in range(NPR):
            length = jnp.where(prompt == k, len_ref[k], length)
        angle = (length + step).astype(F32) * freq_ref[...]
        cos_ref[...] = jnp.cos(angle)
        sin_ref[...] = jnp.where(lane < 64, -jnp.sin(angle), jnp.sin(angle))
        key = iota((128, 128), 0)
        query = iota((128, 128), 1)
        query_row = query - lax.shift_right_logical(query * 171, 12) * OWN
        prompt = lax.shift_right_logical(query_row * 43, 8)
        length = jnp.zeros((128, 128), jnp.int32)
        start = jnp.zeros((128, 128), jnp.int32)
        offset = jnp.int32(0)
        for k in range(NPR):
            length = jnp.where(prompt == k, len_ref[k], length)
            start = jnp.where(prompt == k, offset, start)
            offset = offset + len_ref[k]
        past_ref[...] = key - start
        length_ref[...] = length

    def project(layer):
        first = ids(14)
        sib = hs[1 - core]
        weights = win.at[layer]
        part = dot(sib, weights[:, PART0:])
        c1s[...] = part.reshape(2, 4, OWN, PART1)
        send(first + 0, c1s.at[other], c1r.at[layer, other], sibling)
        part = dot(sib, weights[:, :PART0])
        for q in range(8):
            c0s[q % 4, q // 4, :, :PART0] = part[OWN * q : OWN * q + OWN]
        send(first + 1, c0s.at[far], c0r.at[layer, far], sibling)
        send(first + 2, c0s.at[ahead], c0r.at[layer, ahead], sibling)
        send(first + 3, c0s.at[behind], c0r.at[layer, behind], sibling)
        send(first + 4, c0s.at[x], c0r.at[layer, x], sibling)
        send(first + 5, c1s.at[y], c1r.at[layer, y], sibling)
        mine = hs[core]
        part = dot(mine, weights[:, PART0:])
        s1[...] = part.reshape(2, 4, OWN, PART1)
        part = dot(mine, weights[:, :PART0])
        for q in range(8):
            s0[q % 4, q // 4, :, :PART0] = part[OWN * q : OWN * q + OWN]

        def core_sum(index, total, came):
            arrived(index, came)
            total[...] = total[...] + came[...]

        core_sum(first + 0, s1.at[other], c1r.at[layer, other])
        send(first + 6, s1.at[other], y1r.at[layer], to_other)
        core_sum(first + 1, s0.at[far], c0r.at[layer, far])
        send(first + 7, s0.at[far], x0relay.at[layer], to_ahead)
        core_sum(first + 2, s0.at[behind], c0r.at[layer, behind])
        send(first + 8, s0.at[behind], x0dir.at[layer], to_behind)
        core_sum(first + 3, s0.at[ahead], c0r.at[layer, ahead])
        core_sum(first + 4, s0.at[x], c0r.at[layer, x])
        core_sum(first + 5, s1.at[y], c1r.at[layer, y])
        if layer == 0:
            gathers[0].cross()
            gathers[0].along(0)
            tables()
        loads[("wout", layer)].wait()
        wout[...] = wpad[layer].T
        arrived(first + 7, x0relay.at[layer])
        s0[ahead] = s0[ahead] + x0relay[layer]
        send(first + 9, s0.at[ahead], x0fin.at[layer], to_ahead)
        arrived(first + 6, y1r.at[layer])
        s1[y] = s1[y] + y1r[layer]
        send(first + 10, s1.at[y, far], x1relay.at[layer], to_ahead)
        send(first + 11, s1.at[y, behind], x1dir.at[layer], to_behind)
        if layer == 0:
            gathers[0].last(0)
            gathers[0].along(1)
        arrived(first + 10, x1relay.at[layer])
        s1[y, ahead] = s1[y, ahead] + x1relay[layer]
        send(first + 12, s1.at[y, ahead], x1fin.at[layer], to_ahead)
        arrived(first + 8, x0dir.at[layer])
        arrived(first + 9, x0fin.at[layer])
        s0[x] = s0[x] + x0dir[layer] + x0fin[layer]
        send(first + 13, s0.at[x, other], y0r.at[layer], to_other)
        if layer == 0:
            gathers[0].last(1)
            gathers[0].core_side(0)
            gathers[0].core_side(1)
        arrived(first + 11, x1dir.at[layer])
        arrived(first + 12, x1fin.at[layer])
        part1 = s1[y, x] + x1dir[layer] + x1fin[layer]
        arrived(first + 13, y0r.at[layer])
        part0 = s0[x, y] + y0r[layer]
        return part0, part1

    def attend(layer, part0, part1):
        inverse = lax.rsqrt(part0[:, PART0:] / WIDTH + EPSILON)
        cosine = cos_ref[...]
        sine = sin_ref[...]

        def rotate(vector):
            return vector * cosine + pltpu.roll(vector, 64, 1) * sine

        blocks = [part0[:, HEAD * h : HEAD * h + HEAD] * inverse for h in range(5)]
        blocks += [part1[:, HEAD * h : HEAD * h + HEAD] * inverse for h in range(5)]
        spare = jnp.zeros((128 - 4 * OWN, HEAD), F32)
        queries = [rotate(block) * HEAD**-0.5 for block in blocks[:HEADS]]
        queries = [jnp.concatenate(queries[4 * half : 4 * half + 4] + [spare], axis=0).T for half in range(2)]
        queries = jnp.concatenate(queries, axis=1)
        first = queries.astype(BF16)
        rest = queries - first.astype(F32)
        second = rest.astype(BF16)
        third = (rest - second.astype(F32)).astype(BF16)
        upper = jnp.concatenate([first, second], axis=0)
        empty = jnp.zeros((128 - OWN, HEAD), F32)
        kv[layer, 16, 0] = jnp.concatenate([rotate(blocks[8]), empty], axis=0).astype(BF16)
        kv[layer, 16, 1] = jnp.concatenate([blocks[9], empty], axis=0).T.astype(BF16)

        def visit(block, count, seen, running):
            peak, total, summed = running
            keys = kv[layer, pl.ds(block, count), 0].reshape(count * 128, HEAD)
            scores = dot(keys, third) + dot(jnp.concatenate([keys, keys], axis=1), upper)
            parts = []
            for i in range(count):
                bias = jnp.where(seen(i), 0.0, NEGATIVE)
                part = scores[128 * i : 128 * i + 128] + jnp.concatenate([bias, bias], axis=1)
                maxima = jnp.max(part, axis=0, keepdims=True)
                weights = jnp.exp(part - maxima)
                sums = jnp.sum(weights, axis=0, keepdims=True)
                parts.append((maxima, sums, dot(kv[layer, block + i, 1], weights.astype(BF16))))
            higher = peak
            for maxima, _, _ in parts:
                higher = jnp.maximum(higher, maxima)
            left = jnp.exp(peak - higher)
            total = total * left
            summed = summed * left
            for maxima, sums, values in parts:
                right = jnp.exp(maxima - higher)
                total = total + sums * right
                summed = summed + values * right
            return higher, total, summed

        key = iota((128, 128), 0)
        query = iota((128, 128), 1)
        query_row = query - lax.shift_right_logical(query * 171, 12) * OWN
        query_sample = lax.shift_right_logical(query_row * 43, 8)
        key_sample = lax.shift_right_logical(key * 43, 8)
        recent = (query_sample == key_sample) & (key <= query_row)
        running = (
            jnp.full((1, 256), NEGATIVE, F32),
            jnp.zeros((1, 256), F32),
            jnp.zeros((HEAD, 256), F32),
        )
        running = visit(16, 1, lambda i: recent, running)

        def prompt_blocks(group, running):
            def seen(i):
                past = past_ref[...] + (group * 4 + i) * 128
                return (past >= 0) & (past < length_ref[...])

            return visit(group * 4, 4, seen, running)

        _, total, summed = lax.fori_loop(0, 4, prompt_blocks, running)
        attention = summed / total
        halves = []
        for half in range(2):
            rows = attention[:, 128 * half : 128 * half + 128].T
            halves.append(jnp.concatenate([rows[OWN * h : OWN * h + OWN] for h in range(4)], axis=1))
        gat[layer, s] = jnp.concatenate(halves, axis=0).astype(BF16)

    def collect(layer):
        gather = Gather(gat.at[layer])
        gather.begin()
        gather.along(0)
        gather.cross()
        gather.last(0)
        gather.along(1)

        def product(half):
            rows = gat[layer, pl.ds(half * 8, 8)].reshape(8 * CHIP, 512)
            upper = dot(rows, wout[:512])
            lower = dot(rows, wout[512:])
            for q in range(4):
                at = 2 * CHIP * q
                block = jnp.concatenate(
                    [
                        upper[at : at + OWN] + lower[at + OWN : at + CHIP],
                        upper[at + CHIP : at + CHIP + OWN] + lower[at + CHIP + OWN : at + 2 * CHIP],
                    ],
                    axis=0,
                )
                ob[half * 4 + q] = pack(block)

        first = ids(7)
        early = (y + z + 1) % 2

        def hand_over(k):
            send(first + k, ob.at[chip_of(ring(-1 - k))], d1r.at[layer, k], partner)

        gather.core_side(0)
        product(y)
        hand_over(early + 2)
        hand_over(early)
        gather.last(1)
        gather.core_side(1)
        product(other)
        hand_over(3 - early)
        hand_over(1 - early)
        if layer == 0:
            begin_prompt(1)
        for k in (early + 2, 3 - early, 1):
            at = ring(k)
            block = ob.at[chip_of(at)]
            arrived(first + k, d1r.at[layer, k])
            block[...] = block[...] + d1r[layer, k]
            send(first + 3 + k, block, d2r.at[layer, k - 1], {"tensor": at})
        arrived(first + 0, d1r.at[layer, 0])
        total = ob[chip_of(z)] + d1r[layer, 0]
        if layer == 0:
            gathers[1].cross()
            gathers[1].along(0)
        for k in (1, 2, 3):
            arrived(first + 3 + k, d2r.at[layer, k - 1])
            total = total + d2r[layer, k - 1]
        return total

    def tensor_gather(buf):
        first = ids(7)
        mine = buf.at[z]
        send(first + 2, mine, mine, {"tensor": ring(3)})
        send(first + 1, mine, mine, {"tensor": ring(-2)})
        send(first + 0, mine, mine, {"tensor": ring(1)})
        send(first + 3, mine, mine, partner)
        for k in (1, 2, 3):
            block = buf.at[ring(k)]
            arrived(first + k - 1, block)
            send(first + 3 + k, block, block, partner)
        for k in (0, 1, 2, 3):
            arrived(first + 3 + k, buf.at[ring(-1 - k)])

    part0, part1 = project(0)
    attend(0, part0, part1)
    stream = pack(hid[pl.ds(pl.multiple_of(chip_of(z) * CHIP, 8), CHIP), :]) + collect(0)
    str1[...] = stream
    tail = unpack_tail(stream)
    lane = iota((CHIP, 128), 1)
    middle0 = stream[:CHIP]
    middle1 = stream[CHIP : 2 * CHIP]
    kept = jnp.where(lane < 64, tail, 0.0)
    squares = jnp.sum(middle0 * middle0 + middle1 * middle1 + kept * kept, axis=1, keepdims=True)
    square1 = squares.astype(BF16).astype(F32)
    square2 = (squares - square1).astype(BF16).astype(F32)
    square3 = squares - square1 - square2
    kept = jnp.where(lane == 64, square1, kept)
    kept = jnp.where(lane == 65, square2, kept)
    kept = jnp.where(lane == 66, square3, kept)
    sg[z] = jnp.concatenate([middle0, middle1, kept], axis=1).astype(BF16)
    tensor_gather(sg)
    gathers[1].last(0)
    gathers[1].along(1)
    drain()

    flip = core == 1
    by_parity = [[], []]
    for q in range(8):
        block = sg[2 * (q % 4) + q // 4].astype(F32)
        sums = jnp.sum(jnp.where(lane >= 64, block[:, 256:], 0.0), axis=1, keepdims=True)
        sums = jnp.broadcast_to(sums, (CHIP, 128))
        s0[q % 4, q // 4, :, PART0:] = jnp.where(flip, sums[OWN:], sums[:OWN])
        c0s[q % 4, q // 4, :, PART0:] = jnp.where(flip, sums[:OWN], sums[OWN:])
        for parity in range(2):
            by_parity[parity].append(block[OWN * parity : OWN * parity + OWN, :COLS])
    for parity in range(2):
        hs[parity] = jnp.concatenate(by_parity[parity], axis=0).astype(BF16)
    loads["win1"].wait()
    part0, part1 = project(1)
    gathers[1].last(1)
    gathers[1].core_side(0)
    gathers[1].core_side(1)
    attend(1, part0, part1)
    fg[z] = str1[...] + collect(1)
    tensor_gather(fg)
    for d in range(8):
        block = fg[d]
        rows = pl.ds(CHIP * chip_of(d), CHIP)
        out_rows[rows, 0:128] = block[:CHIP]
        out_rows[rows, 128:256] = block[CHIP : 2 * CHIP]
        out_rows[rows, 256:384] = unpack_tail(block)
    out_ref[...] = out_rows[...].T[:COLS]
    drain()


def on_device(hidden_in, prompt_len, cached_prompt_keys, cached_prompt_values, query_key_value_weight, w_out):
    keys = cached_prompt_keys.reshape(LAYERS, 128, HEAD)
    values = cached_prompt_values.reshape(LAYERS, 128, HEAD)
    half = np.power(ROPE_BASE, -2.0 * np.arange(64) / HEAD)
    freq = jnp.asarray(np.concatenate([half, half])[None, :], F32)
    vmem = pltpu.VMEM
    scratch = [
        vmem((PAD, ROWS), F32),
        vmem((ROWS, PAD), F32),
        vmem((LAYERS, COLS, 1280), BF16),
        vmem((LAYERS, PAD, 1024), BF16),
        vmem((1024, PAD), BF16),
        vmem((LAYERS, 128, HEAD), BF16),
        vmem((LAYERS, 17, 2, 128, HEAD), BF16),
        vmem((2, 192, COLS), BF16),
        vmem((4, 2, OWN, WIDE0), F32),
        vmem((2, 4, OWN, PART1), F32),
        vmem((LAYERS, 4, 2, OWN, WIDE0), F32),
        vmem((LAYERS, 2, 4, OWN, PART1), F32),
        vmem((4, 2, OWN, WIDE0), F32),
        vmem((2, 4, OWN, PART1), F32),
        vmem((LAYERS, 2, OWN, WIDE0), F32),
        vmem((LAYERS, 2, OWN, WIDE0), F32),
        vmem((LAYERS, 2, OWN, WIDE0), F32),
        vmem((LAYERS, OWN, PART1), F32),
        vmem((LAYERS, OWN, PART1), F32),
        vmem((LAYERS, OWN, PART1), F32),
        vmem((LAYERS, 4, OWN, PART1), F32),
        vmem((LAYERS, OWN, WIDE0), F32),
        vmem((128, 128), jnp.int32),
        vmem((128, 128), jnp.int32),
        vmem((OWN, 128), F32),
        vmem((OWN, 128), F32),
        vmem((LAYERS, 16, CHIP, 512), BF16),
        vmem((8, PACKED, 128), F32),
        vmem((LAYERS, 4, PACKED, 128), F32),
        vmem((LAYERS, 3, PACKED, 128), F32),
        vmem((8, CHIP, PAD), BF16),
        vmem((8, PACKED, 128), F32),
        vmem((PACKED, 128), F32),
        vmem((ROWS, PAD), F32),
        pltpu.SemaphoreType.DMA((9,)),
        pltpu.SemaphoreType.DMA((COPIES,)),
        pltpu.SemaphoreType.DMA((COPIES,)),
    ]
    hbm = pl.BlockSpec(memory_space=pl.ANY)
    out = pl.pallas_call(
        kernel,
        out_shape=jax.ShapeDtypeStruct((COLS, ROWS), F32),
        in_specs=[
            pl.BlockSpec(memory_space=pltpu.SMEM),
            pl.BlockSpec(memory_space=pltpu.VMEM),
            hbm, hbm, hbm, hbm, hbm,
        ],
        out_specs=pl.BlockSpec(memory_space=pltpu.VMEM),
        scratch_shapes=scratch,
        compiler_params=pltpu.CompilerParams(
            collective_id=0, has_side_effects=True, vmem_limit_bytes=60 * 1024 * 1024
        ),
        name="two_layers",
    )(prompt_len, freq, hidden_in.T, keys, values, query_key_value_weight, w_out.transpose(0, 2, 1))
    return out.T


def solution(mesh):
    return jax.shard_map(
        on_device,
        mesh=mesh,
        in_specs=(
            P("prompt", "sample"),
            P("prompt"),
            P(None, ("prompt", "sample"), "tensor", None),
            P(None, ("prompt", "sample"), "tensor", None),
            P(None, "sample", "tensor"),
            P(None, "tensor", "sample"),
        ),
        out_specs=P("prompt", "sample"),
        check_vma=False,
    )
```

```python
import jax
import jax.numpy as jnp
import numpy as np
from jax import lax
from jax.experimental import pallas as pl
from jax.experimental.pallas import tpu as pltpu
from jax.sharding import PartitionSpec as P

STEPS = 6
NPR = 4
HEADS = 8
HEAD = 128
LAYERS = 2
ROPE_BASE = 1000000.0
EPSILON = 1e-06
NEGATIVE = -1e30
WIDTH = 5120
ROWS = 384
OWN = 24
CHIP = 48
COLS = 320
PAD = 384
PART0 = 640
PART1 = 640
WIDE0 = PART0 + 128
COPIES = 128
MESH = pl.DeviceIdType.MESH
F32 = jnp.float32
BF16 = jnp.bfloat16


def dot(a, b):
    return jnp.dot(a, b, preferred_element_type=F32)


def iota(shape, axis):
    return lax.broadcasted_iota(jnp.int32, shape, axis)


def kernel(
    len_ref, freq_ref, hid_hbm, key_hbm, val_hbm, win_hbm, wout_hbm, out_ref,
    hid_across, hid, win, wpad, wout, val, kv, hs, s0, s1,
    x0relay, x0dir, x0fin, x1relay, x1dir, x1fin, y1r, y0r,
    past_ref, length_ref, cos_ref, sin_ref, gat, ob, d1r, d2r, sg, fg, fs, str1, out_rows, out_cols,
    load_sem, send_sem, recv_sem,
):
    s = lax.axis_index("sample")
    z = lax.axis_index("tensor")
    core = s % 2
    chip = s // 2
    x = chip % 4
    y = chip // 4
    other = 1 - y
    sigma = 1 - 2 * core
    ahead = (x + sigma + 4) % 4
    behind = (x - sigma + 4) % 4
    far = (x + 2) % 4
    delta = 2 * ((z + core) % 2) - 1

    def place(py, px, pc):
        return (py * 4 + px) * 2 + pc

    def ring(step):
        return (z + delta * step + 8) % 8

    def chip_of(at):
        return (at % 2) * 4 + at // 2

    sibling = {"sample": place(y, x, 1 - core)}
    to_ahead = {"sample": place(y, ahead, core)}
    to_behind = {"sample": place(y, behind, core)}
    to_other = {"sample": place(other, x, core)}
    to_other_ahead = {"sample": place(other, ahead, core)}
    to_other_behind = {"sample": place(other, behind, core)}
    partner = {"tensor": ring(-1)}

    used = [0]
    pending = []

    def ids(count):
        first = used[0]
        used[0] += count
        return first

    def send(index, src, dst, device):
        copy = pltpu.make_async_remote_copy(
            src_ref=src, dst_ref=dst, send_sem=send_sem.at[index], recv_sem=recv_sem.at[index],
            device_id=device, device_id_type=MESH,
        )
        copy.start()
        pending.append(copy)

    def arrived(index, ref):
        pltpu.make_async_remote_copy(
            src_ref=ref, dst_ref=ref, send_sem=send_sem.at[index], recv_sem=recv_sem.at[index],
            device_id=sibling, device_id_type=MESH,
        ).wait_recv()

    def drain():
        for copy in pending:
            copy.wait_send()
        pending.clear()

    loads = {}

    def load(name, index, src, dst):
        loads[name] = pltpu.make_async_copy(src, dst, load_sem.at[index])
        loads[name].start()

    load("hid", 0, hid_hbm, hid_across.at[core])
    load(("win", 0), 1, win_hbm.at[0], win.at[0, core])
    for layer in range(LAYERS):
        load(("key", layer), 2 + 2 * layer, key_hbm.at[layer], kv.at[layer, s, 0])
        load(("val", layer), 3 + 2 * layer, val_hbm.at[layer], val.at[layer])
    load(("wout", 0), 6, wout_hbm.at[0], wpad.at[0, core])
    load(("win", 1), 7, win_hbm.at[1], win.at[1, core])
    load(("wout", 1), 8, wout_hbm.at[1], wpad.at[1, core])

    barrier = pltpu.get_barrier_semaphore()
    near = [sibling, to_ahead, to_behind, to_other, to_other_ahead, to_other_behind]
    near += [{"tensor": ring(step)} for step in (-1, 1, 2, -2, 3)]
    for device in near:
        pl.semaphore_signal(barrier, inc=1, device_id=device, device_id_type=MESH)
    pl.semaphore_wait(barrier, len(near))

    shared = ids(5)
    send(shared + 0, hid_hbm, hid_across.at[core], sibling)
    send(shared + 1, win_hbm.at[0], win.at[0, core], sibling)

    class Gather:
        def __init__(self, buf):
            self.buf = buf
            self.first = ids(15)

        def put(self, number, py, px, device, pc=None):
            block = self.buf.at[place(py, px, core)]
            send(self.first + number, block, block, device)

        def get(self, number, py, px, pc=None):
            where = place(py, px, core if pc is None else pc)
            arrived(self.first + number, self.buf.at[where])

        def begin(self):
            self.put(0, y, x, to_other)
            self.put(1, y, x, to_ahead)
            self.put(2, y, x, to_behind)
            self.put(7, y, x, sibling)

        def cross(self):
            self.get(0, other, x)
            self.put(4, other, x, to_ahead)
            self.put(5, other, x, to_behind)
            self.put(11, other, x, sibling)

        def along(self, half):
            py, at, near_core = (y, 1, 8) if half == 0 else (other, 4, 12)
            self.get(at, py, behind)
            self.put(at + 2, py, behind, to_ahead)
            self.put(near_core, py, behind, sibling)
            self.get(at + 1, py, ahead)
            self.put(near_core + 1, py, ahead, sibling)

        def last(self, half):
            py, at, near_core = (y, 3, 10) if half == 0 else (other, 6, 14)
            self.get(at, py, far)
            self.put(near_core, py, far, sibling)

        def core_side(self, half):
            py, at = (y, 7) if half == 0 else (other, 11)
            for number, px in enumerate((x, ahead, behind, far)):
                self.get(at + number, py, px, 1 - core)

    gathers = [Gather(kv.at[layer]) for layer in range(LAYERS)]

    def begin_prompt(layer):
        loads[("key", layer)].wait()
        loads[("val", layer)].wait()
        kv[layer, s, 1] = val[layer].astype(F32).T.astype(BF16)
        gathers[layer].begin()

    begin_prompt(0)

    send(shared + 2, wout_hbm.at[0], wpad.at[0, core], sibling)
    send(shared + 3, win_hbm.at[1], win.at[1, core], sibling)
    send(shared + 4, wout_hbm.at[1], wpad.at[1, core], sibling)

    def my_rows(q):
        return pl.ds(pl.multiple_of(q * CHIP + core * OWN, 8), OWN)

    loads["hid"].wait()
    arrived(shared + 0, hid_across.at[1 - core])
    hid[...] = hid_across[...].reshape(2 * COLS, ROWS).T
    pieces = [hid[my_rows(q), :] for q in range(8)]
    hs[...] = jnp.concatenate(pieces, axis=0).astype(BF16)
    for q in range(8):
        squares = jnp.sum(pieces[q] * pieces[q], axis=1, keepdims=True)
        s0[q % 4, q // 4, :, PART0:] = jnp.broadcast_to(squares, (OWN, 128))

    def tables():
        row = iota((OWN, 128), 0)
        lane = iota((OWN, 128), 1)
        prompt = lax.shift_right_logical(row * 43, 8)
        step = row - prompt * STEPS
        length = jnp.zeros((OWN, 128), jnp.int32)
        for k in range(NPR):
            length = jnp.where(prompt == k, len_ref[k], length)
        angle = (length + step).astype(F32) * freq_ref[...]
        cos_ref[...] = jnp.cos(angle)
        sin_ref[...] = jnp.where(lane < 64, -jnp.sin(angle), jnp.sin(angle))
        key = iota((128, 128), 0)
        query = iota((128, 128), 1)
        query_row = query - lax.shift_right_logical(query * 171, 12) * OWN
        prompt = lax.shift_right_logical(query_row * 43, 8)
        length = jnp.zeros((128, 128), jnp.int32)
        start = jnp.zeros((128, 128), jnp.int32)
        offset = jnp.int32(0)
        for k in range(NPR):
            length = jnp.where(prompt == k, len_ref[k], length)
            start = jnp.where(prompt == k, offset, start)
            offset = offset + len_ref[k]
        past_ref[...] = key - start
        length_ref[...] = length

    def project(layer):
        first = ids(8)
        loads[("win", layer)].wait()
        arrived(shared + 1 + 2 * layer, win.at[layer, 1 - core])
        rows = hs[...]
        part = dot(rows, win[layer, :, :, PART0:].reshape(2 * COLS, PART1))
        s1[...] = part.reshape(2, 4, OWN, PART1)
        send(first + 0, s1.at[other], y1r.at[layer], to_other)
        part = dot(rows, win[layer, :, :, :PART0].reshape(2 * COLS, PART0))
        for q in range(8):
            s0[q % 4, q // 4, :, :PART0] = part[OWN * q : OWN * q + OWN]
        send(first + 1, s0.at[far], x0relay.at[layer], to_ahead)
        send(first + 2, s0.at[behind], x0dir.at[layer], to_behind)
        if layer == 0:
            gathers[0].cross()
            gathers[0].along(0)
            tables()
        loads[("wout", layer)].wait()
        arrived(shared + 2 + 2 * layer, wpad.at[layer, 1 - core])
        wout[...] = wpad[layer].reshape(2 * COLS, 1024).T
        arrived(first + 1, x0relay.at[layer])
        s0[ahead] = s0[ahead] + x0relay[layer]
        send(first + 3, s0.at[ahead], x0fin.at[layer], to_ahead)
        arrived(first + 0, y1r.at[layer])
        s1[y] = s1[y] + y1r[layer]
        send(first + 4, s1.at[y, far], x1relay.at[layer], to_ahead)
        send(first + 5, s1.at[y, behind], x1dir.at[layer], to_behind)
        if layer == 0:
            gathers[0].last(0)
            gathers[0].along(1)
        arrived(first + 4, x1relay.at[layer])
        s1[y, ahead] = s1[y, ahead] + x1relay[layer]
        send(first + 6, s1.at[y, ahead], x1fin.at[layer], to_ahead)
        arrived(first + 2, x0dir.at[layer])
        arrived(first + 3, x0fin.at[layer])
        s0[x] = s0[x] + x0dir[layer] + x0fin[layer]
        send(first + 7, s0.at[x, other], y0r.at[layer], to_other)
        if layer == 0:
            gathers[0].last(1)
            gathers[0].core_side(0)
            gathers[0].core_side(1)
        arrived(first + 5, x1dir.at[layer])
        arrived(first + 6, x1fin.at[layer])
        part1 = s1[y, x] + x1dir[layer] + x1fin[layer]
        arrived(first + 7, y0r.at[layer])
        part0 = s0[x, y] + y0r[layer]
        return part0, part1

    def attend(layer, part0, part1):
        inverse = lax.rsqrt(part0[:, PART0:] / WIDTH + EPSILON)
        cosine = cos_ref[...]
        sine = sin_ref[...]

        def rotate(vector):
            return vector * cosine + pltpu.roll(vector, 64, 1) * sine

        blocks = [part0[:, HEAD * h : HEAD * h + HEAD] * inverse for h in range(5)]
        blocks += [part1[:, HEAD * h : HEAD * h + HEAD] * inverse for h in range(5)]
        spare = jnp.zeros((128 - 4 * OWN, HEAD), F32)
        queries = [rotate(block) * HEAD**-0.5 for block in blocks[:HEADS]]
        queries = [jnp.concatenate(queries[4 * half : 4 * half + 4] + [spare], axis=0).T for half in range(2)]
        queries = jnp.concatenate(queries, axis=1)
        first = queries.astype(BF16)
        rest = queries - first.astype(F32)
        second = rest.astype(BF16)
        third = (rest - second.astype(F32)).astype(BF16)
        upper = jnp.concatenate([first, second], axis=0)
        empty = jnp.zeros((128 - OWN, HEAD), F32)
        kv[layer, 16, 0] = jnp.concatenate([rotate(blocks[8]), empty], axis=0).astype(BF16)
        kv[layer, 16, 1] = jnp.concatenate([blocks[9], empty], axis=0).T.astype(BF16)

        def visit(block, count, seen, running):
            peak, total, summed = running
            keys = kv[layer, pl.ds(block, count), 0].reshape(count * 128, HEAD)
            scores = dot(keys, third) + dot(jnp.concatenate([keys, keys], axis=1), upper)
            parts = []
            for i in range(count):
                bias = jnp.where(seen(i), 0.0, NEGATIVE)
                part = scores[128 * i : 128 * i + 128] + jnp.concatenate([bias, bias], axis=1)
                maxima = jnp.max(part, axis=0, keepdims=True)
                weights = jnp.exp(part - maxima)
                sums = jnp.sum(weights, axis=0, keepdims=True)
                parts.append((maxima, sums, dot(kv[layer, block + i, 1], weights.astype(BF16))))
            higher = peak
            for maxima, _, _ in parts:
                higher = jnp.maximum(higher, maxima)
            left = jnp.exp(peak - higher)
            total = total * left
            summed = summed * left
            for maxima, sums, values in parts:
                right = jnp.exp(maxima - higher)
                total = total + sums * right
                summed = summed + values * right
            return higher, total, summed

        key = iota((128, 128), 0)
        query = iota((128, 128), 1)
        query_row = query - lax.shift_right_logical(query * 171, 12) * OWN
        query_sample = lax.shift_right_logical(query_row * 43, 8)
        key_sample = lax.shift_right_logical(key * 43, 8)
        recent = (query_sample == key_sample) & (key <= query_row)
        running = (
            jnp.full((1, 256), NEGATIVE, F32),
            jnp.zeros((1, 256), F32),
            jnp.zeros((HEAD, 256), F32),
        )
        running = visit(16, 1, lambda i: recent, running)

        def prompt_blocks(group, running):
            def seen(i):
                past = past_ref[...] + (group * 4 + i) * 128
                return (past >= 0) & (past < length_ref[...])

            return visit(group * 4, 4, seen, running)

        _, total, summed = lax.fori_loop(0, 4, prompt_blocks, running)
        attention = summed / total
        halves = []
        for half in range(2):
            rows = attention[:, 128 * half : 128 * half + 128].T
            halves.append(jnp.concatenate([rows[OWN * h : OWN * h + OWN] for h in range(4)], axis=1))
        gat[layer, chip] = jnp.concatenate(halves, axis=0).astype(BF16)

    def collect(layer):
        at = ids(7)
        buf = gat.at[layer]
        mine = buf.at[chip]
        send(at + 0, mine, mine, to_ahead)
        send(at + 1, mine, mine, to_behind)
        send(at + 3, mine, mine, to_other_ahead)
        send(at + 4, mine, mine, to_other_behind)
        send(at + 2, mine, mine, to_other)

        def came(number, py, px):
            block = buf.at[py * 4 + px]
            arrived(at + number, block)
            return block

        block = came(0, y, behind)
        send(at + 5, block, block, to_ahead)
        block = came(3, other, behind)
        send(at + 6, block, block, to_ahead)

        def product(half):
            blocks = gat[layer, pl.ds(half * 4, 4)].astype(F32)
            rows = [jnp.concatenate([blocks[q, :OWN], blocks[q, OWN:]], axis=1) for q in range(4)]
            result = dot(jnp.concatenate(rows, axis=0).astype(BF16), wout[...])
            for q in range(4):
                ob[half * 4 + q] = result[OWN * q : OWN * q + OWN]

        first = ids(7)
        early = (y + z + 1) % 2

        def hand_over(k):
            send(first + k, ob.at[chip_of(ring(-1 - k))], d1r.at[layer, k], partner)

        came(1, y, ahead)
        came(5, y, far)
        product(y)
        hand_over(early + 2)
        hand_over(early)
        came(2, other, x)
        came(4, other, ahead)
        came(6, other, far)
        product(other)
        hand_over(3 - early)
        hand_over(1 - early)
        if layer == 0:
            begin_prompt(1)
        for k in (early + 2, 3 - early, 1):
            at = ring(k)
            block = ob.at[chip_of(at)]
            arrived(first + k, d1r.at[layer, k])
            block[...] = block[...] + d1r[layer, k]
            send(first + 3 + k, block, d2r.at[layer, k - 1], {"tensor": at})
        arrived(first + 0, d1r.at[layer, 0])
        total = ob[chip_of(z)] + d1r[layer, 0]
        if layer == 0:
            gathers[1].cross()
            gathers[1].along(0)
        for k in (1, 2, 3):
            arrived(first + 3 + k, d2r.at[layer, k - 1])
            total = total + d2r[layer, k - 1]
        return total

    def tensor_gather(buf, held=lambda at: None):
        first = ids(7)
        mine = buf.at[z]
        send(first + 2, mine, mine, {"tensor": ring(3)})
        send(first + 1, mine, mine, {"tensor": ring(-2)})
        send(first + 0, mine, mine, {"tensor": ring(1)})
        send(first + 3, mine, mine, partner)
        held(z)
        for k in (1, 2, 3):
            block = buf.at[ring(k)]
            arrived(first + k - 1, block)
            send(first + 3 + k, block, block, partner)
            held(ring(k))
        for k in (0, 1, 2, 3):
            arrived(first + 3 + k, buf.at[ring(-1 - k)])
            held(ring(-1 - k))

    part0, part1 = project(0)
    attend(0, part0, part1)
    stream = hid[my_rows(chip_of(z)), :] + collect(0)
    str1[...] = stream
    squares = jnp.sum(stream * stream, axis=1, keepdims=True)
    square1 = squares.astype(BF16).astype(F32)
    square2 = (squares - square1).astype(BF16).astype(F32)
    square3 = squares - square1 - square2
    diagonal = iota((OWN, 128), 0) == iota((OWN, 128), 1)
    line = iota((8, 128), 0)
    extra = jnp.zeros((8, 128), F32)
    for i, term in enumerate((square1, square2, square3)):
        across = jnp.sum(jnp.where(diagonal, term, 0.0), axis=0, keepdims=True)
        extra = jnp.where(line == i, across, extra)
    tiles = [stream[:, 128 * t : 128 * t + 128] for t in range(5)]
    sg[z] = jnp.concatenate(tiles + [extra], axis=0).astype(BF16)
    tensor_gather(sg)
    gathers[1].last(0)
    gathers[1].along(1)
    drain()

    pieces = []
    for q in range(8):
        block = sg[2 * (q % 4) + q // 4].astype(F32)
        across = jnp.sum(block[5 * OWN :], axis=0, keepdims=True)
        squares = jnp.sum(jnp.where(diagonal, across, 0.0), axis=1, keepdims=True)
        s0[q % 4, q // 4, :, PART0:] = jnp.broadcast_to(squares, (OWN, 128))
        pieces.append(jnp.concatenate([block[OWN * t : OWN * t + OWN] for t in range(5)], axis=1))
    hs[...] = jnp.concatenate(pieces, axis=0).astype(BF16)
    part0, part1 = project(1)
    gathers[1].last(1)
    gathers[1].core_side(0)
    gathers[1].core_side(1)
    attend(1, part0, part1)
    stream = str1[...] + collect(1)
    for t in range(5):
        fg[z, t] = stream[:, 128 * t : 128 * t + 128]
    crossing = ids(8)

    def hand_across(at):
        send(crossing + at, fg.at[at, pl.ds(2 - 2 * core, 3)], fs.at[at], sibling)

    tensor_gather(fg, hand_across)
    for at in range(8):
        for t in range(3):
            out_rows[my_rows(chip_of(at)), 128 * t : 128 * t + 128] = fg[at, 2 * core + t]
    for at in range(8):
        arrived(crossing + at, fs.at[at])
        theirs = pl.ds(pl.multiple_of(chip_of(at) * CHIP + (1 - core) * OWN, 8), OWN)
        for t in range(3):
            out_rows[theirs, 128 * t : 128 * t + 128] = fs[at, t]
    out_cols[...] = out_rows[...].T
    out_ref[...] = out_cols[pl.ds(pl.multiple_of(core * 64, 8), COLS), :]
    drain()


def on_device(hidden_in, prompt_len, cached_prompt_keys, cached_prompt_values, query_key_value_weight, w_out):
    keys = cached_prompt_keys.reshape(LAYERS, 128, HEAD)
    values = cached_prompt_values.reshape(LAYERS, 128, HEAD)
    half = np.power(ROPE_BASE, -2.0 * np.arange(64) / HEAD)
    freq = jnp.asarray(np.concatenate([half, half])[None, :], F32)
    vmem = pltpu.VMEM
    scratch = [
        vmem((2, COLS, ROWS), F32),
        vmem((ROWS, 2 * COLS), F32),
        vmem((LAYERS, 2, COLS, 1280), BF16),
        vmem((LAYERS, 2, COLS, 1024), BF16),
        vmem((1024, 2 * COLS), BF16),
        vmem((LAYERS, 128, HEAD), BF16),
        vmem((LAYERS, 17, 2, 128, HEAD), BF16),
        vmem((8 * OWN, 2 * COLS), BF16),
        vmem((4, 2, OWN, WIDE0), F32),
        vmem((2, 4, OWN, PART1), F32),
        vmem((LAYERS, 2, OWN, WIDE0), F32),
        vmem((LAYERS, 2, OWN, WIDE0), F32),
        vmem((LAYERS, 2, OWN, WIDE0), F32),
        vmem((LAYERS, OWN, PART1), F32),
        vmem((LAYERS, OWN, PART1), F32),
        vmem((LAYERS, OWN, PART1), F32),
        vmem((LAYERS, 4, OWN, PART1), F32),
        vmem((LAYERS, OWN, WIDE0), F32),
        vmem((128, 128), jnp.int32),
        vmem((128, 128), jnp.int32),
        vmem((OWN, 128), F32),
        vmem((OWN, 128), F32),
        vmem((LAYERS, 8, CHIP, 512), BF16),
        vmem((8, OWN, 2 * COLS), F32),
        vmem((LAYERS, 4, OWN, 2 * COLS), F32),
        vmem((LAYERS, 3, OWN, 2 * COLS), F32),
        vmem((8, 128, 128), BF16),
        vmem((8, 5, OWN, 128), F32),
        vmem((8, 3, OWN, 128), F32),
        vmem((OWN, 2 * COLS), F32),
        vmem((ROWS, PAD), F32),
        vmem((PAD, ROWS), F32),
        pltpu.SemaphoreType.DMA((9,)),
        pltpu.SemaphoreType.DMA((COPIES,)),
        pltpu.SemaphoreType.DMA((COPIES,)),
    ]
    hbm = pl.BlockSpec(memory_space=pl.ANY)
    out = pl.pallas_call(
        kernel,
        out_shape=jax.ShapeDtypeStruct((COLS, ROWS), F32),
        in_specs=[
            pl.BlockSpec(memory_space=pltpu.SMEM),
            pl.BlockSpec(memory_space=pltpu.VMEM),
            hbm, hbm, hbm, hbm, hbm,
        ],
        out_specs=pl.BlockSpec(memory_space=pltpu.VMEM),
        scratch_shapes=scratch,
        compiler_params=pltpu.CompilerParams(
            collective_id=0, has_side_effects=True, vmem_limit_bytes=60 * 1024 * 1024
        ),
        name="two_layers",
    )(prompt_len, freq, hidden_in.T, keys, values, query_key_value_weight, w_out.transpose(0, 2, 1))
    return out.T


def solution(mesh):
    return jax.shard_map(
        on_device,
        mesh=mesh,
        in_specs=(
            P("prompt", "sample"),
            P("prompt"),
            P(None, ("prompt", "sample"), "tensor", None),
            P(None, ("prompt", "sample"), "tensor", None),
            P(None, "sample", "tensor"),
            P(None, "tensor", "sample"),
        ),
        out_specs=P("prompt", "sample"),
        check_vma=False,
    )
```

```python
import jax
import jax.numpy as jnp
import numpy as np
from jax import lax
from jax.experimental import pallas as pl
from jax.experimental.pallas import tpu as pltpu
from jax.sharding import PartitionSpec as P

STEPS = 6
NPR = 4
HEADS = 8
HEAD = 128
LAYERS = 2
ROPE_BASE = 1000000.0
EPSILON = 1e-06
NEGATIVE = -1e30
WIDTH = 5120
ROWS = 384
OWN = 24
CHIP = 48
COLS = 320
PAD = 384
PART0 = 640
PART1 = 640
WIDE0 = PART0 + 128
COPIES = 176
GROUPS = (16, 8)
MESH = pl.DeviceIdType.MESH
F32 = jnp.float32
BF16 = jnp.bfloat16


def dot(a, b):
    return jnp.dot(a, b, preferred_element_type=F32)


def iota(shape, axis):
    return lax.broadcasted_iota(jnp.int32, shape, axis)


def kernel(
    len_ref, freq_ref, hid_hbm, key_hbm, val_hbm, win_hbm, wout_hbm, out_ref,
    hid_across, hid, win, wpad, wout, val, kv, cos_ref, sin_ref, past_ref, length_ref, newest, out_rows, out_cols,
    *grouped,
):
    load_sem, send_sem, recv_sem = grouped[-3:]
    s = lax.axis_index("sample")
    z = lax.axis_index("tensor")
    core = s % 2
    chip = s // 2
    x = chip % 4
    y = chip // 4
    other = 1 - y
    sigma = 1 - 2 * core
    ahead = (x + sigma + 4) % 4
    behind = (x - sigma + 4) % 4
    far = (x + 2) % 4
    delta = 2 * ((z + core) % 2) - 1

    def place(py, px, pc):
        return (py * 4 + px) * 2 + pc

    def ring(step):
        return (z + delta * step + 8) % 8

    def chip_of(at):
        return (at % 2) * 4 + at // 2

    sibling = {"sample": place(y, x, 1 - core)}
    to_ahead = {"sample": place(y, ahead, core)}
    to_behind = {"sample": place(y, behind, core)}
    to_other = {"sample": place(other, x, core)}
    to_other_ahead = {"sample": place(other, ahead, core)}
    to_other_behind = {"sample": place(other, behind, core)}
    partner = {"tensor": ring(-1)}

    used = [0]
    pending = [[], [], []]

    def ids(count):
        first = used[0]
        used[0] += count
        return first

    def send(index, src, dst, device, chain=2):
        copy = pltpu.make_async_remote_copy(
            src_ref=src, dst_ref=dst, send_sem=send_sem.at[index], recv_sem=recv_sem.at[index],
            device_id=device, device_id_type=MESH,
        )
        copy.start()
        pending[chain].append(copy)

    def arrived(index, ref):
        pltpu.make_async_remote_copy(
            src_ref=ref, dst_ref=ref, send_sem=send_sem.at[index], recv_sem=recv_sem.at[index],
            device_id=sibling, device_id_type=MESH,
        ).wait_recv()

    def drain(chain):
        for copy in pending[chain]:
            copy.wait_send()
        pending[chain].clear()

    loads = {}

    def load(name, index, src, dst):
        loads[name] = pltpu.make_async_copy(src, dst, load_sem.at[index])
        loads[name].start()

    load("hid", 0, hid_hbm, hid_across.at[core])
    load(("win", 0), 1, win_hbm.at[0], win.at[0, core])
    for layer in range(LAYERS):
        load(("key", layer), 2 + 2 * layer, key_hbm.at[layer], kv.at[layer, s, 0])
        load(("val", layer), 3 + 2 * layer, val_hbm.at[layer], val.at[layer])
    load(("wout", 0), 6, wout_hbm.at[0], wpad.at[0, core])
    load(("win", 1), 7, win_hbm.at[1], win.at[1, core])
    load(("wout", 1), 8, wout_hbm.at[1], wpad.at[1, core])

    barrier = pltpu.get_barrier_semaphore()
    near = [sibling, to_ahead, to_behind, to_other, to_other_ahead, to_other_behind]
    near += [{"tensor": ring(step)} for step in (-1, 1, 2, -2, 3)]
    for device in near:
        pl.semaphore_signal(barrier, inc=1, device_id=device, device_id_type=MESH)
    pl.semaphore_wait(barrier, len(near))

    shared = ids(5)
    send(shared + 0, hid_hbm, hid_across.at[core], sibling)
    send(shared + 1, win_hbm.at[0], win.at[0, core], sibling)

    class Gather:
        def __init__(self, buf):
            self.buf = buf
            self.first = ids(15)

        def put(self, number, py, px, device, pc=None):
            block = self.buf.at[place(py, px, core)]
            send(self.first + number, block, block, device)

        def get(self, number, py, px, pc=None):
            where = place(py, px, core if pc is None else pc)
            arrived(self.first + number, self.buf.at[where])

        def begin(self):
            self.put(0, y, x, to_other)
            self.put(1, y, x, to_ahead)
            self.put(2, y, x, to_behind)
            self.put(7, y, x, sibling)

        def cross(self):
            self.get(0, other, x)
            self.put(4, other, x, to_ahead)
            self.put(5, other, x, to_behind)
            self.put(11, other, x, sibling)

        def along(self, half):
            py, at, near_core = (y, 1, 8) if half == 0 else (other, 4, 12)
            self.get(at, py, behind)
            self.put(at + 2, py, behind, to_ahead)
            self.put(near_core, py, behind, sibling)
            self.get(at + 1, py, ahead)
            self.put(near_core + 1, py, ahead, sibling)

        def last(self, half):
            py, at, near_core = (y, 3, 10) if half == 0 else (other, 6, 14)
            self.get(at, py, far)
            self.put(near_core, py, far, sibling)

        def core_side(self, half):
            py, at = (y, 7) if half == 0 else (other, 11)
            for number, px in enumerate((x, ahead, behind, far)):
                self.get(at + number, py, px, 1 - core)

    gathers = [Gather(kv.at[layer]) for layer in range(LAYERS)]

    def begin_prompt(layer):
        loads[("key", layer)].wait()
        loads[("val", layer)].wait()
        kv[layer, s, 1] = val[layer].astype(F32).T.astype(BF16)
        gathers[layer].begin()

    begin_prompt(0)

    send(shared + 2, wout_hbm.at[0], wpad.at[0, core], sibling)
    send(shared + 3, win_hbm.at[1], win.at[1, core], sibling)
    send(shared + 4, wout_hbm.at[1], wpad.at[1, core], sibling)

    def my_rows(q):
        return pl.ds(pl.multiple_of(q * CHIP + core * OWN, 8), OWN)

    loads["hid"].wait()
    arrived(shared + 0, hid_across.at[1 - core])
    hid[...] = hid_across[...].reshape(2 * COLS, ROWS).T
    buffers = [grouped[len(NAMES) * g : len(NAMES) * g + len(NAMES)] for g in range(2)]
    buffers = [dict(zip(NAMES, refs)) for refs in buffers]
    for q in range(8):
        piece = hid[my_rows(q), :]
        buffers[0]["rows"][q] = jnp.concatenate([piece[6 * j : 6 * j + 4] for j in range(NPR)], axis=0)
        buffers[1]["rows"][q] = jnp.concatenate([piece[6 * j + 4 : 6 * j + 6] for j in range(NPR)], axis=0)

    def sample_and_step(row, g):
        sample = lax.shift_right_logical(row, 2 - g)
        return sample, row - sample * (4 - 2 * g) + 4 * g

    def tables(g):
        count = GROUPS[g]
        lane = iota((count, 128), 1)
        sample, step = sample_and_step(iota((count, 128), 0), g)
        length = jnp.zeros((count, 128), jnp.int32)
        for k in range(NPR):
            length = jnp.where(sample == k, len_ref[k], length)
        angle = (length + step).astype(F32) * freq_ref[...]
        cos_ref[g, :count] = jnp.cos(angle)
        sin_ref[g, :count] = jnp.where(lane < 64, -jnp.sin(angle), jnp.sin(angle))
        key = iota((128, 128), 0)
        query = iota((128, 128), 1)
        sample, _ = sample_and_step(query % count, g)
        length = jnp.zeros((128, 128), jnp.int32)
        start = jnp.zeros((128, 128), jnp.int32)
        offset = jnp.int32(0)
        for k in range(NPR):
            length = jnp.where(sample == k, len_ref[k], length)
            start = jnp.where(sample == k, offset, start)
            offset = offset + len_ref[k]
        past_ref[g] = key - start
        length_ref[g] = length

    def recent(g):
        key = iota((128, 128), 0)
        sample, step = sample_and_step(iota((128, 128), 1) % GROUPS[g], g)
        early_sample, early_step = sample_and_step(key, 0)
        late_sample, late_step = sample_and_step(key - 16, 1)
        seen = (key < 16) & (early_sample == sample) & (early_step <= step)
        return seen | ((key >= 16) & (key < 24) & (late_sample == sample) & (late_step <= step))

    def attend(layer, g, part0, part1):
        count = GROUPS[g]
        inverse = lax.rsqrt(part0[:, PART0:] / WIDTH + EPSILON)
        cosine = cos_ref[g, :count]
        sine = sin_ref[g, :count]

        def rotate(vector):
            return vector * cosine + pltpu.roll(vector, 64, 1) * sine

        blocks = [part0[:, HEAD * h : HEAD * h + HEAD] * inverse for h in range(5)]
        blocks += [part1[:, HEAD * h : HEAD * h + HEAD] * inverse for h in range(5)]
        queries = [rotate(block) * HEAD**-0.5 for block in blocks[:HEADS]]
        if g == 1:
            queries.append(jnp.zeros((64, HEAD), F32))
        queries = jnp.concatenate(queries, axis=0).T
        first = queries.astype(BF16)
        rest = queries - first.astype(F32)
        second = rest.astype(BF16)
        third = (rest - second.astype(F32)).astype(BF16)
        upper = jnp.concatenate([first, second], axis=0)
        if g == 0:
            newest[...] = blocks[9]
            empty = jnp.zeros((112, HEAD), F32)
            kv[layer, 16, 0] = jnp.concatenate([rotate(blocks[8]), empty], axis=0).astype(BF16)
            kv[layer, 16, 1] = jnp.concatenate([blocks[9], empty], axis=0).T.astype(BF16)
        else:
            empty = jnp.zeros((8, HEAD), F32)
            kv[layer, 16, 0, 16:32] = jnp.concatenate([rotate(blocks[8]), empty], axis=0).astype(BF16)
            empty = jnp.zeros((104, HEAD), F32)
            kv[layer, 16, 1] = jnp.concatenate([newest[...], blocks[9], empty], axis=0).T.astype(BF16)

        def visit(block, count, seen, running):
            peak, total, summed = running
            keys = kv[layer, pl.ds(block, count), 0].reshape(count * 128, HEAD)
            scores = dot(keys, third) + dot(jnp.concatenate([keys, keys], axis=1), upper)
            parts = []
            for i in range(count):
                part = scores[128 * i : 128 * i + 128] + jnp.where(seen(i), 0.0, NEGATIVE)
                maxima = jnp.max(part, axis=0, keepdims=True)
                weights = jnp.exp(part - maxima)
                sums = jnp.sum(weights, axis=0, keepdims=True)
                parts.append((maxima, sums, dot(kv[layer, block + i, 1], weights.astype(BF16))))
            higher = peak
            for maxima, _, _ in parts:
                higher = jnp.maximum(higher, maxima)
            left = jnp.exp(peak - higher)
            total = total * left
            summed = summed * left
            for maxima, sums, values in parts:
                right = jnp.exp(maxima - higher)
                total = total + sums * right
                summed = summed + values * right
            return higher, total, summed

        running = (jnp.full((1, 128), NEGATIVE, F32), jnp.zeros((1, 128), F32), jnp.zeros((HEAD, 128), F32))
        running = visit(16, 1, lambda i: recent(g), running)

        def prompt_blocks(group, running):
            def seen(i):
                past = past_ref[g] + (group * 4 + i) * 128
                return (past >= 0) & (past < length_ref[g])

            return visit(group * 4, 4, seen, running)

        _, total, summed = lax.fori_loop(0, 4, prompt_blocks, running)
        rows = (summed / total).T
        heads = [rows[count * h : count * h + count] for h in range(HEADS)]
        if g == 0:
            return jnp.concatenate(heads, axis=1).astype(BF16)
        halves = [jnp.concatenate(heads[:4], axis=1), jnp.concatenate(heads[4:], axis=1)]
        return jnp.concatenate(halves, axis=0).astype(BF16)

    def tensor_gather(buf, chain, held=lambda at: None):
        first = ids(7)
        mine = buf.at[z]
        send(first + 2, mine, mine, {"tensor": ring(3)}, chain)
        send(first + 1, mine, mine, {"tensor": ring(-2)}, chain)
        send(first + 0, mine, mine, {"tensor": ring(1)}, chain)
        send(first + 3, mine, mine, partner, chain)
        held(z)
        yield
        for k in (1, 2, 3):
            block = buf.at[ring(k)]
            arrived(first + k - 1, block)
            send(first + 3 + k, block, block, partner, chain)
            held(ring(k))
        yield
        for k in (0, 1, 2, 3):
            arrived(first + 3 + k, buf.at[ring(-1 - k)])
            held(ring(-1 - k))

    def chain(g):
        count = GROUPS[g]
        refs = buffers[g]
        s0, s1, own = refs["s0"], refs["s1"], refs["rows"]
        gat, ob = refs["gat"], refs["ob"]
        diagonal = iota((count, 128), 0) == iota((count, 128), 1)

        def put(index, src, dst, device):
            send(index, src, dst, device, g)

        for layer in range(LAYERS):
            pieces = []
            for q in range(8):
                if layer == 0:
                    piece = own[q]
                    squares = jnp.sum(piece * piece, axis=1, keepdims=True)
                else:
                    block = refs["sg"][2 * (q % 4) + q // 4].astype(F32)
                    across = jnp.sum(block[5 * count :], axis=0, keepdims=True)
                    squares = jnp.sum(jnp.where(diagonal, across, 0.0), axis=1, keepdims=True)
                    piece = jnp.concatenate([block[count * t : count * t + count] for t in range(5)], axis=1)
                s0[q % 4, q // 4, :, PART0:] = jnp.broadcast_to(squares, (count, 128))
                pieces.append(piece)
            rows = jnp.concatenate(pieces, axis=0).astype(BF16)

            first = ids(8)
            if g == 0:
                loads[("win", layer)].wait()
                arrived(shared + 1 + 2 * layer, win.at[layer, 1 - core])
            x0relay, x0dir, x0fin = (refs[name].at[layer] for name in ("x0relay", "x0dir", "x0fin"))
            x1relay, x1dir, x1fin = (refs[name].at[layer] for name in ("x1relay", "x1dir", "x1fin"))
            y1r, y0r = refs["y1r"].at[layer], refs["y0r"].at[layer]
            part = dot(rows, win[layer, :, :, PART0:].reshape(2 * COLS, PART1))
            s1[...] = part.reshape(2, 4, count, PART1)
            put(first + 0, s1.at[other], y1r, to_other)
            part = dot(rows, win[layer, :, :, :PART0].reshape(2 * COLS, PART0))
            for q in range(8):
                s0[q % 4, q // 4, :, :PART0] = part[count * q : count * q + count]
            put(first + 1, s0.at[far], x0relay, to_ahead)
            put(first + 2, s0.at[behind], x0dir, to_behind)
            yield
            if g == 0:
                if layer == 0:
                    gathers[0].cross()
                    gathers[0].along(0)
                    tables(0)
                    tables(1)
                loads[("wout", layer)].wait()
                arrived(shared + 2 + 2 * layer, wpad.at[layer, 1 - core])
                wout[layer] = wpad[layer].reshape(2 * COLS, 1024).T
            arrived(first + 1, x0relay)
            s0[ahead] = s0[ahead] + x0relay[...]
            put(first + 3, s0.at[ahead], x0fin, to_ahead)
            arrived(first + 0, y1r)
            s1[y] = s1[y] + y1r[...]
            put(first + 4, s1.at[y, far], x1relay, to_ahead)
            put(first + 5, s1.at[y, behind], x1dir, to_behind)
            yield
            if layer == 0 and g == 0:
                gathers[0].last(0)
                gathers[0].along(1)
            arrived(first + 4, x1relay)
            s1[y, ahead] = s1[y, ahead] + x1relay[...]
            put(first + 6, s1.at[y, ahead], x1fin, to_ahead)
            arrived(first + 2, x0dir)
            arrived(first + 3, x0fin)
            s0[x] = s0[x] + x0dir[...] + x0fin[...]
            put(first + 7, s0.at[x, other], y0r, to_other)
            yield
            if g == 0:
                gathers[layer].last(1)
                gathers[layer].core_side(0)
                gathers[layer].core_side(1)
            arrived(first + 5, x1dir)
            arrived(first + 6, x1fin)
            part1 = s1[y, x] + x1dir[...] + x1fin[...]
            arrived(first + 7, y0r)
            part0 = s0[x, y] + y0r[...]
            gat[layer, chip] = attend(layer, g, part0, part1)

            first = ids(7)
            mine = gat.at[layer, chip]
            put(first + 0, mine, mine, to_ahead)
            put(first + 1, mine, mine, to_behind)
            put(first + 3, mine, mine, to_other_ahead)
            put(first + 4, mine, mine, to_other_behind)
            put(first + 2, mine, mine, to_other)
            yield
            places = ((0, y, behind), (3, other, behind), (1, y, ahead), (2, other, x), (4, other, ahead))
            places += ((5, y, far), (6, other, far))
            for number, py, px in places[:2]:
                block = gat.at[layer, py * 4 + px]
                arrived(first + number, block)
                put(first + (5 if number == 0 else 6), block, block, to_ahead)
            yield
            for number, py, px in places[2:]:
                arrived(first + number, gat.at[layer, py * 4 + px])
            if g == 0:
                rows = gat[layer].reshape(8 * count, 1024)
            else:
                blocks = gat[layer].astype(F32)
                rows = [jnp.concatenate([blocks[q, :count], blocks[q, count:]], axis=1) for q in range(8)]
                rows = jnp.concatenate(rows, axis=0).astype(BF16)
            ob[...] = dot(rows, wout[layer]).reshape(8, count, 2 * COLS)

            first = ids(7)
            d1r, d2r = refs["d1r"], refs["d2r"]
            for k in (3, 2, 1, 0):
                put(first + k, ob.at[chip_of(ring(-1 - k))], d1r.at[layer, k], partner)
            if layer == 0 and g == 1:
                begin_prompt(1)
            yield
            for k in (3, 2, 1):
                at = ring(k)
                block = ob.at[chip_of(at)]
                arrived(first + k, d1r.at[layer, k])
                block[...] = block[...] + d1r[layer, k]
                put(first + 3 + k, block, d2r.at[layer, k - 1], {"tensor": at})
            arrived(first + 0, d1r.at[layer, 0])
            stream = own[chip_of(z)] + ob[chip_of(z)] + d1r[layer, 0]
            if layer == 0 and g == 1:
                gathers[1].cross()
                gathers[1].along(0)
            yield
            for k in (1, 2, 3):
                arrived(first + 3 + k, d2r.at[layer, k - 1])
                stream = stream + d2r[layer, k - 1]
            tiles = [stream[:, 128 * t : 128 * t + 128] for t in range(5)]
            if layer == 0:
                own[chip_of(z)] = stream
                squares = jnp.sum(stream * stream, axis=1, keepdims=True)
                square1 = squares.astype(BF16).astype(F32)
                square2 = (squares - square1).astype(BF16).astype(F32)
                square3 = squares - square1 - square2
                line = iota((count, 128), 0)
                extra = jnp.zeros((count, 128), F32)
                for i, term in enumerate((square1, square2, square3)):
                    across = jnp.sum(jnp.where(diagonal, term, 0.0), axis=0, keepdims=True)
                    extra = jnp.where(line == i, across, extra)
                refs["sg"][z] = jnp.concatenate(tiles + [extra], axis=0).astype(BF16)
                yield from tensor_gather(refs["sg"], g)
                if g == 1:
                    gathers[1].last(0)
                    gathers[1].along(1)
                drain(g)
            else:
                fg, fs = refs["fg"], refs["fs"]
                for t in range(5):
                    fg[z, t] = tiles[t]
                crossing = ids(8)
                refs["crossing"] = crossing

                def hand_across(at):
                    put(crossing + at, fg.at[at, pl.ds(2 - 2 * core, 3)], fs.at[at], sibling)

                yield from tensor_gather(fg, g, hand_across)
                yield

    waiting = [chain(0), chain(1)]
    while waiting:
        for each in list(waiting):
            if next(each, "end") == "end":
                waiting.remove(each)

    def in_order(early, late):
        parts = []
        for j in range(NPR):
            parts += [early[4 * j : 4 * j + 4], late[2 * j : 2 * j + 2]]
        return jnp.concatenate(parts, axis=0)

    for at in range(8):
        for t in range(3):
            both = [buffers[g]["fg"][at, 2 * core + t] for g in range(2)]
            out_rows[my_rows(chip_of(at)), 128 * t : 128 * t + 128] = in_order(*both)
    for at in range(8):
        for g in range(2):
            arrived(buffers[g]["crossing"] + at, buffers[g]["fs"].at[at])
        theirs = pl.ds(pl.multiple_of(chip_of(at) * CHIP + (1 - core) * OWN, 8), OWN)
        for t in range(3):
            both = [buffers[g]["fs"][at, t] for g in range(2)]
            out_rows[theirs, 128 * t : 128 * t + 128] = in_order(*both)
    out_cols[...] = out_rows[...].T
    out_ref[...] = out_cols[pl.ds(pl.multiple_of(core * 64, 8), COLS), :]
    for each in range(3):
        drain(each)


NAMES = (
    "rows", "s0", "s1", "x0relay", "x0dir", "x0fin", "x1relay", "x1dir", "x1fin", "y1r", "y0r",
    "gat", "ob", "d1r", "d2r", "sg", "fg", "fs",
)


def group_scratch(count):
    vmem = pltpu.VMEM
    return [
        vmem((8, count, 2 * COLS), F32),
        vmem((4, 2, count, WIDE0), F32),
        vmem((2, 4, count, PART1), F32),
        *[vmem((LAYERS, 2, count, WIDE0), F32)] * 3,
        *[vmem((LAYERS, count, PART1), F32)] * 3,
        vmem((LAYERS, 4, count, PART1), F32),
        vmem((LAYERS, count, WIDE0), F32),
        vmem((LAYERS, 8, 16, 64 * count), BF16),
        vmem((8, count, 2 * COLS), F32),
        vmem((LAYERS, 4, count, 2 * COLS), F32),
        vmem((LAYERS, 3, count, 2 * COLS), F32),
        vmem((8, 6 * count, 128), BF16),
        vmem((8, 5, count, 128), F32),
        vmem((8, 3, count, 128), F32),
    ]


def on_device(hidden_in, prompt_len, cached_prompt_keys, cached_prompt_values, query_key_value_weight, w_out):
    keys = cached_prompt_keys.reshape(LAYERS, 128, HEAD)
    values = cached_prompt_values.reshape(LAYERS, 128, HEAD)
    half = np.power(ROPE_BASE, -2.0 * np.arange(64) / HEAD)
    freq = jnp.asarray(np.concatenate([half, half])[None, :], F32)
    vmem = pltpu.VMEM
    scratch = [
        vmem((2, COLS, ROWS), F32),
        vmem((ROWS, 2 * COLS), F32),
        vmem((LAYERS, 2, COLS, 1280), BF16),
        vmem((LAYERS, 2, COLS, 1024), BF16),
        vmem((LAYERS, 1024, 2 * COLS), BF16),
        vmem((LAYERS, 128, HEAD), BF16),
        vmem((LAYERS, 17, 2, 128, HEAD), BF16),
        vmem((2, 16, 128), F32),
        vmem((2, 16, 128), F32),
        vmem((2, 128, 128), jnp.int32),
        vmem((2, 128, 128), jnp.int32),
        vmem((16, HEAD), F32),
        vmem((ROWS, PAD), F32),
        vmem((PAD, ROWS), F32),
        *group_scratch(GROUPS[0]),
        *group_scratch(GROUPS[1]),
        pltpu.SemaphoreType.DMA((9,)),
        pltpu.SemaphoreType.DMA((COPIES,)),
        pltpu.SemaphoreType.DMA((COPIES,)),
    ]
    hbm = pl.BlockSpec(memory_space=pl.ANY)
    out = pl.pallas_call(
        kernel,
        out_shape=jax.ShapeDtypeStruct((COLS, ROWS), F32),
        in_specs=[
            pl.BlockSpec(memory_space=pltpu.SMEM),
            pl.BlockSpec(memory_space=pltpu.VMEM),
            hbm, hbm, hbm, hbm, hbm,
        ],
        out_specs=pl.BlockSpec(memory_space=pltpu.VMEM),
        scratch_shapes=scratch,
        compiler_params=pltpu.CompilerParams(
            collective_id=0, has_side_effects=True, vmem_limit_bytes=60 * 1024 * 1024
        ),
        name="two_layers",
    )(prompt_len, freq, hidden_in.T, keys, values, query_key_value_weight, w_out.transpose(0, 2, 1))
    return out.T


def solution(mesh):
    return jax.shard_map(
        on_device,
        mesh=mesh,
        in_specs=(
            P("prompt", "sample"),
            P("prompt"),
            P(None, ("prompt", "sample"), "tensor", None),
            P(None, ("prompt", "sample"), "tensor", None),
            P(None, "sample", "tensor"),
            P(None, "tensor", "sample"),
        ),
        out_specs=P("prompt", "sample"),
        check_vma=False,
    )
```

```python
import jax
import jax.numpy as jnp
import numpy as np
from jax import lax
from jax.experimental import pallas as pl
from jax.experimental.pallas import tpu as pltpu
from jax.sharding import PartitionSpec as P

STEPS = 6
NPR = 4
HEADS = 8
HEAD = 128
LAYERS = 2
ROPE_BASE = 1000000.0
EPSILON = 1e-06
NEGATIVE = -1e30
WIDTH = 5120
ROWS = 384
OWN = 24
CHIP = 48
COLS = 320
PAD = 384
PART0 = 640
PART1 = 640
WIDE0 = PART0 + 128
COPIES = 192
GROUPS = (16, 8)
MESH = pl.DeviceIdType.MESH
F32 = jnp.float32
BF16 = jnp.bfloat16


def dot(a, b):
    return jnp.dot(a, b, preferred_element_type=F32)


def iota(shape, axis):
    return lax.broadcasted_iota(jnp.int32, shape, axis)


def kernel(
    len_ref, freq_ref, hid_hbm, key_hbm, val_hbm, win_hbm, wout_hbm, out_ref,
    hid_across, hid, win, wpad, wout, val, kv, cos_ref, sin_ref, past_ref, length_ref, newest, out_rows, out_cols,
    *grouped,
):
    load_sem, send_sem, recv_sem = grouped[-3:]
    s = lax.axis_index("sample")
    z = lax.axis_index("tensor")
    core = s % 2
    chip = s // 2
    x = chip % 4
    y = chip // 4
    other = 1 - y
    sigma = 1 - 2 * core
    ahead = (x + sigma + 4) % 4
    behind = (x - sigma + 4) % 4
    far = (x + 2) % 4
    delta = 2 * ((z + core) % 2) - 1

    def place(py, px, pc):
        return (py * 4 + px) * 2 + pc

    def ring(step):
        return (z + delta * step + 8) % 8

    def chip_of(at):
        return (at % 2) * 4 + at // 2

    sibling = {"sample": place(y, x, 1 - core)}
    to_ahead = {"sample": place(y, ahead, core)}
    to_behind = {"sample": place(y, behind, core)}
    to_other = {"sample": place(other, x, core)}
    to_other_ahead = {"sample": place(other, ahead, core)}
    to_other_behind = {"sample": place(other, behind, core)}
    partner = {"tensor": ring(-1)}

    used = [0]
    pending = [[], [], []]

    def ids(count):
        first = used[0]
        used[0] += count
        return first

    def send(index, src, dst, device, chain=2):
        copy = pltpu.make_async_remote_copy(
            src_ref=src, dst_ref=dst, send_sem=send_sem.at[index], recv_sem=recv_sem.at[index],
            device_id=device, device_id_type=MESH,
        )
        copy.start()
        pending[chain].append(copy)

    def arrived(index, ref):
        pltpu.make_async_remote_copy(
            src_ref=ref, dst_ref=ref, send_sem=send_sem.at[index], recv_sem=recv_sem.at[index],
            device_id=sibling, device_id_type=MESH,
        ).wait_recv()

    def drain(chain):
        for copy in pending[chain]:
            copy.wait_send()
        pending[chain].clear()

    loads = {}

    def load(name, index, src, dst):
        loads[name] = pltpu.make_async_copy(src, dst, load_sem.at[index])
        loads[name].start()

    load("hid", 0, hid_hbm, hid_across.at[core])
    load(("win", 0), 1, win_hbm.at[0], win.at[0, core])
    for layer in range(LAYERS):
        load(("key", layer), 2 + 2 * layer, key_hbm.at[layer], kv.at[layer, s, 0])
        load(("val", layer), 3 + 2 * layer, val_hbm.at[layer], val.at[layer])
    load(("wout", 0), 6, wout_hbm.at[0], wpad.at[0, core])
    load(("win", 1), 7, win_hbm.at[1], win.at[1, core])
    load(("wout", 1), 8, wout_hbm.at[1], wpad.at[1, core])

    barrier = pltpu.get_barrier_semaphore()
    near = [sibling, to_ahead, to_behind, to_other, to_other_ahead, to_other_behind]
    near += [{"tensor": ring(step)} for step in (-1, 1, 2, -2, 3)]
    for device in near:
        pl.semaphore_signal(barrier, inc=1, device_id=device, device_id_type=MESH)
    pl.semaphore_wait(barrier, len(near))

    shared = ids(6)
    send(shared + 0, hid_hbm, hid_across.at[core], sibling)
    last_half, first_half = pl.ds(PART0, PART1), pl.ds(0, PART0)
    send(shared + 1, win_hbm.at[0, :, last_half], win.at[0, core, :, last_half], sibling)
    send(shared + 5, win_hbm.at[0, :, first_half], win.at[0, core, :, first_half], sibling)

    class Gather:
        def __init__(self, buf):
            self.buf = buf
            self.first = ids(15)

        def put(self, number, py, px, device, pc=None):
            block = self.buf.at[place(py, px, core)]
            send(self.first + number, block, block, device)

        def get(self, number, py, px, pc=None):
            where = place(py, px, core if pc is None else pc)
            arrived(self.first + number, self.buf.at[where])

        def begin(self):
            self.put(0, y, x, to_other)
            self.put(1, y, x, to_ahead)
            self.put(2, y, x, to_behind)
            self.put(7, y, x, sibling)

        def cross(self):
            self.get(0, other, x)
            self.put(4, other, x, to_ahead)
            self.put(5, other, x, to_behind)
            self.put(11, other, x, sibling)

        def along(self, half):
            py, at, near_core = (y, 1, 8) if half == 0 else (other, 4, 12)
            self.get(at, py, behind)
            self.put(at + 2, py, behind, to_ahead)
            self.put(near_core, py, behind, sibling)
            self.get(at + 1, py, ahead)
            self.put(near_core + 1, py, ahead, sibling)

        def last(self, half):
            py, at, near_core = (y, 3, 10) if half == 0 else (other, 6, 14)
            self.get(at, py, far)
            self.put(near_core, py, far, sibling)

        def core_side(self, half):
            py, at = (y, 7) if half == 0 else (other, 11)
            for number, px in enumerate((x, ahead, behind, far)):
                self.get(at + number, py, px, 1 - core)

    gathers = [Gather(kv.at[layer]) for layer in range(LAYERS)]

    def begin_prompt(layer):
        loads[("key", layer)].wait()
        loads[("val", layer)].wait()
        kv[layer, s, 1] = val[layer].astype(F32).T.astype(BF16)
        gathers[layer].begin()

    begin_prompt(0)

    send(shared + 2, wout_hbm.at[0], wpad.at[0, core], sibling)
    send(shared + 3, win_hbm.at[1], win.at[1, core], sibling)
    send(shared + 4, wout_hbm.at[1], wpad.at[1, core], sibling)

    def my_rows(q):
        return pl.ds(pl.multiple_of(q * CHIP + core * OWN, 8), OWN)

    loads["hid"].wait()
    arrived(shared + 0, hid_across.at[1 - core])
    hid[...] = hid_across[...].reshape(2 * COLS, ROWS).T
    buffers = [grouped[len(NAMES) * g : len(NAMES) * g + len(NAMES)] for g in range(2)]
    buffers = [dict(zip(NAMES, refs)) for refs in buffers]
    for q in range(8):
        piece = hid[my_rows(q), :]
        buffers[0]["rows"][q] = jnp.concatenate([piece[6 * j : 6 * j + 4] for j in range(NPR)], axis=0)
        buffers[1]["rows"][q] = jnp.concatenate([piece[6 * j + 4 : 6 * j + 6] for j in range(NPR)], axis=0)

    gathers[0].cross()
    gathers[0].along(0)

    def turn(layer, quarter):
        if quarter == 0:
            loads[("wout", layer)].wait()
            arrived(shared + 2 + 2 * layer, wpad.at[layer, 1 - core])
        part = slice(256 * quarter, 256 * quarter + 256)
        wout[layer, part] = wpad[layer, :, :, part].reshape(2 * COLS, 256).T

    def sample_and_step(row, g):
        sample = lax.shift_right_logical(row, 2 - g)
        return sample, row - sample * (4 - 2 * g) + 4 * g

    def tables(g):
        count = GROUPS[g]
        lane = iota((count, 128), 1)
        sample, step = sample_and_step(iota((count, 128), 0), g)
        length = jnp.zeros((count, 128), jnp.int32)
        for k in range(NPR):
            length = jnp.where(sample == k, len_ref[k], length)
        angle = (length + step).astype(F32) * freq_ref[...]
        cos_ref[g, :count] = jnp.cos(angle)
        sin_ref[g, :count] = jnp.where(lane < 64, -jnp.sin(angle), jnp.sin(angle))
        key = iota((128, 128), 0)
        query = iota((128, 128), 1)
        sample, _ = sample_and_step(query % count, g)
        length = jnp.zeros((128, 128), jnp.int32)
        start = jnp.zeros((128, 128), jnp.int32)
        offset = jnp.int32(0)
        for k in range(NPR):
            length = jnp.where(sample == k, len_ref[k], length)
            start = jnp.where(sample == k, offset, start)
            offset = offset + len_ref[k]
        past_ref[g] = key - start
        length_ref[g] = length

    def recent(g):
        key = iota((128, 128), 0)
        sample, step = sample_and_step(iota((128, 128), 1) % GROUPS[g], g)
        early_sample, early_step = sample_and_step(key, 0)
        late_sample, late_step = sample_and_step(key - 16, 1)
        seen = (key < 16) & (early_sample == sample) & (early_step <= step)
        return seen | ((key >= 16) & (key < 24) & (late_sample == sample) & (late_step <= step))

    def attend(layer, g, part0, part1):
        count = GROUPS[g]
        inverse = lax.rsqrt(part0[:, PART0:] / WIDTH + EPSILON)
        cosine = cos_ref[g, :count]
        sine = sin_ref[g, :count]

        def rotate(vector):
            return vector * cosine + pltpu.roll(vector, 64, 1) * sine

        blocks = [part0[:, HEAD * h : HEAD * h + HEAD] * inverse for h in range(5)]
        blocks += [part1[:, HEAD * h : HEAD * h + HEAD] * inverse for h in range(5)]
        queries = [rotate(block) * HEAD**-0.5 for block in blocks[:HEADS]]
        if g == 1:
            queries.append(jnp.zeros((64, HEAD), F32))
        queries = jnp.concatenate(queries, axis=0).T
        first = queries.astype(BF16)
        rest = queries - first.astype(F32)
        second = rest.astype(BF16)
        third = (rest - second.astype(F32)).astype(BF16)
        upper = jnp.concatenate([first, second], axis=0)
        if g == 0:
            newest[...] = blocks[9]
            empty = jnp.zeros((112, HEAD), F32)
            kv[layer, 16, 0] = jnp.concatenate([rotate(blocks[8]), empty], axis=0).astype(BF16)
            kv[layer, 16, 1] = jnp.concatenate([blocks[9], empty], axis=0).T.astype(BF16)
        else:
            empty = jnp.zeros((8, HEAD), F32)
            kv[layer, 16, 0, 16:32] = jnp.concatenate([rotate(blocks[8]), empty], axis=0).astype(BF16)
            empty = jnp.zeros((104, HEAD), F32)
            kv[layer, 16, 1] = jnp.concatenate([newest[...], blocks[9], empty], axis=0).T.astype(BF16)

        def visit(block, count, seen, running):
            peak, total, summed = running
            keys = kv[layer, pl.ds(block, count), 0].reshape(count * 128, HEAD)
            scores = dot(keys, third) + dot(jnp.concatenate([keys, keys], axis=1), upper)
            parts = []
            for i in range(count):
                part = scores[128 * i : 128 * i + 128] + jnp.where(seen(i), 0.0, NEGATIVE)
                maxima = jnp.max(part, axis=0, keepdims=True)
                weights = jnp.exp(part - maxima)
                sums = jnp.sum(weights, axis=0, keepdims=True)
                parts.append((maxima, sums, dot(kv[layer, block + i, 1], weights.astype(BF16))))
            higher = peak
            for maxima, _, _ in parts:
                higher = jnp.maximum(higher, maxima)
            left = jnp.exp(peak - higher)
            total = total * left
            summed = summed * left
            for maxima, sums, values in parts:
                right = jnp.exp(maxima - higher)
                total = total + sums * right
                summed = summed + values * right
            return higher, total, summed

        running = (jnp.full((1, 128), NEGATIVE, F32), jnp.zeros((1, 128), F32), jnp.zeros((HEAD, 128), F32))
        running = visit(16, 1, lambda i: recent(g), running)

        def prompt_blocks(group, running):
            def seen(i):
                past = past_ref[g] + (group * 4 + i) * 128
                return (past >= 0) & (past < length_ref[g])

            return visit(group * 4, 4, seen, running)

        _, total, summed = lax.fori_loop(0, 4, prompt_blocks, running)
        rows = (summed / total).T
        heads = [rows[count * h : count * h + count] for h in range(HEADS)]
        if g == 0:
            return jnp.concatenate(heads, axis=1).astype(BF16)
        halves = [jnp.concatenate(heads[:4], axis=1), jnp.concatenate(heads[4:], axis=1)]
        return jnp.concatenate(halves, axis=0).astype(BF16)

    def tensor_gather(buf, chain, held=lambda at: None):
        first = ids(7)
        mine = buf.at[z]
        send(first + 2, mine, mine, {"tensor": ring(3)}, chain)
        send(first + 1, mine, mine, {"tensor": ring(-2)}, chain)
        send(first + 0, mine, mine, {"tensor": ring(1)}, chain)
        send(first + 3, mine, mine, partner, chain)
        held(z)
        yield
        for k in (1, 2, 3):
            block = buf.at[ring(k)]
            arrived(first + k - 1, block)
            send(first + 3 + k, block, block, partner, chain)
            held(ring(k))
        yield
        for k in (0, 1, 2, 3):
            arrived(first + 3 + k, buf.at[ring(-1 - k)])
            held(ring(-1 - k))

    def chain(g):
        count = GROUPS[g]
        refs = buffers[g]
        s0, s1, own = refs["s0"], refs["s1"], refs["rows"]
        gat, ob = refs["gat"], refs["ob"]
        diagonal = iota((count, 128), 0) == iota((count, 128), 1)

        def put(index, src, dst, device):
            send(index, src, dst, device, g)

        for layer in range(LAYERS):
            pieces = []
            for q in range(8):
                if layer == 0:
                    piece = own[q]
                    squares = jnp.sum(piece * piece, axis=1, keepdims=True)
                else:
                    block = refs["sg"][2 * (q % 4) + q // 4].astype(F32)
                    across = jnp.sum(block[5 * count :], axis=0, keepdims=True)
                    squares = jnp.sum(jnp.where(diagonal, across, 0.0), axis=1, keepdims=True)
                    piece = jnp.concatenate([block[count * t : count * t + count] for t in range(5)], axis=1)
                s0[q % 4, q // 4, :, PART0:] = jnp.broadcast_to(squares, (count, 128))
                pieces.append(piece)
            rows = jnp.concatenate(pieces, axis=0).astype(BF16)

            first = ids(14)
            if g == 0:
                loads[("win", layer)].wait()
                if layer == 0:
                    arrived(shared + 1, win.at[0, 1 - core, :, last_half])
                else:
                    arrived(shared + 3, win.at[1, 1 - core])
            x0relay, x0dir, x0fin = (refs[name].at[layer] for name in ("x0relay", "x0dir", "x0fin"))
            x1relay, x1dir, x1fin = (refs[name].at[layer] for name in ("x1relay", "x1dir", "x1fin"))
            y1r, y0r = refs["y1r"].at[layer], refs["y0r"].at[layer]
            part = dot(rows, win[layer, :, :, PART0:].reshape(2 * COLS, PART1))
            s1[...] = part.reshape(2, 4, count, PART1)
            for number, px in enumerate((far, behind, ahead, x)):
                put(first + number, s1.at[other, px], y1r.at[px], to_other)
            if g == 0 and layer == 0:
                arrived(shared + 5, win.at[0, 1 - core, :, first_half])
            part = dot(rows, win[layer, :, :, :PART0].reshape(2 * COLS, PART0))
            for q in range(8):
                s0[q % 4, q // 4, :, :PART0] = part[count * q : count * q + count]
            for number, py in enumerate((other, y)):
                put(first + 4 + number, s0.at[far, py], x0relay.at[py], to_ahead)
                put(first + 6 + number, s0.at[behind, py], x0dir.at[py], to_behind)
            if g == 1 and layer == 0:
                tables(0)
                tables(1)
                turn(0, 0)
            elif g == 1:
                turn(1, 2)
            yield
            if g == 0 and layer == 0:
                gathers[0].last(0)
                gathers[0].along(1)

            def pass_on(number, py):
                arrived(first + 4 + number, x0relay.at[py])
                s0[ahead, py] = s0[ahead, py] + x0relay[py]
                put(first + 8 + number, s0.at[ahead, py], x0fin.at[py], to_ahead)

            pass_on(0, other)
            for number, px, to, device in ((0, far, x1relay, to_ahead), (1, behind, x1dir, to_behind)):
                arrived(first + number, y1r.at[px])
                s1[y, px] = s1[y, px] + y1r[px]
                put(first + 10 + number, s1.at[y, px], to, device)
            pass_on(1, y)
            if g == 1 and layer == 0:
                turn(0, 1)
                turn(0, 2)
            elif g == 1:
                turn(1, 3)
            yield
            if g == 0 and layer == 0:
                gathers[0].last(1)
            arrived(first + 6, x0dir.at[other])
            arrived(first + 8, x0fin.at[other])
            s0[x, other] = s0[x, other] + x0dir[other] + x0fin[other]
            put(first + 13, s0.at[x, other], y0r, to_other)
            arrived(first + 10, x1relay)
            arrived(first + 2, y1r.at[ahead])
            s1[y, ahead] = s1[y, ahead] + y1r[ahead] + x1relay[...]
            put(first + 12, s1.at[y, ahead], x1fin, to_ahead)
            if g == 1 and layer == 0:
                turn(0, 3)
            yield
            if g == 0:
                if layer == 1:
                    gathers[1].last(1)
                gathers[layer].core_side(0)
                gathers[layer].core_side(1)
            arrived(first + 3, y1r.at[x])
            arrived(first + 11, x1dir)
            arrived(first + 12, x1fin)
            part1 = s1[y, x] + y1r[x] + x1dir[...] + x1fin[...]
            arrived(first + 7, x0dir.at[y])
            arrived(first + 9, x0fin.at[y])
            part0 = s0[x, y] + x0dir[y] + x0fin[y]
            arrived(first + 13, y0r)
            part0 = part0 + y0r[...]
            gat[layer, chip] = attend(layer, g, part0, part1)

            first = ids(7)
            mine = gat.at[layer, chip]
            put(first + 0, mine, mine, to_ahead)
            put(first + 1, mine, mine, to_behind)
            put(first + 3, mine, mine, to_other_ahead)
            put(first + 4, mine, mine, to_other_behind)
            put(first + 2, mine, mine, to_other)
            yield
            places = ((0, y, behind), (3, other, behind), (1, y, ahead), (2, other, x), (4, other, ahead))
            places += ((5, y, far), (6, other, far))
            for number, py, px in places[:2]:
                block = gat.at[layer, py * 4 + px]
                arrived(first + number, block)
                put(first + (5 if number == 0 else 6), block, block, to_ahead)
            yield
            for number, py, px in places[2:]:
                arrived(first + number, gat.at[layer, py * 4 + px])
            if g == 0:
                rows = gat[layer].reshape(8 * count, 1024)
            else:
                blocks = gat[layer].astype(F32)
                rows = [jnp.concatenate([blocks[q, :count], blocks[q, count:]], axis=1) for q in range(8)]
                rows = jnp.concatenate(rows, axis=0).astype(BF16)
            ob[...] = dot(rows, wout[layer]).reshape(8, count, 2 * COLS)

            first = ids(7)
            d1r, d2r = refs["d1r"], refs["d2r"]
            for k in (3, 2, 1, 0):
                put(first + k, ob.at[chip_of(ring(-1 - k))], d1r.at[layer, k], partner)
            if layer == 0 and g == 1:
                begin_prompt(1)
                turn(1, 0)
            yield
            for k in (3, 2, 1):
                at = ring(k)
                block = ob.at[chip_of(at)]
                arrived(first + k, d1r.at[layer, k])
                block[...] = block[...] + d1r[layer, k]
                put(first + 3 + k, block, d2r.at[layer, k - 1], {"tensor": at})
            arrived(first + 0, d1r.at[layer, 0])
            stream = own[chip_of(z)] + ob[chip_of(z)] + d1r[layer, 0]
            if layer == 0 and g == 1:
                gathers[1].cross()
                gathers[1].along(0)
                turn(1, 1)
            yield
            for k in (1, 2, 3):
                arrived(first + 3 + k, d2r.at[layer, k - 1])
                stream = stream + d2r[layer, k - 1]
            tiles = [stream[:, 128 * t : 128 * t + 128] for t in range(5)]
            if layer == 0:
                own[chip_of(z)] = stream
                squares = jnp.sum(stream * stream, axis=1, keepdims=True)
                square1 = squares.astype(BF16).astype(F32)
                square2 = (squares - square1).astype(BF16).astype(F32)
                square3 = squares - square1 - square2
                line = iota((count, 128), 0)
                extra = jnp.zeros((count, 128), F32)
                for i, term in enumerate((square1, square2, square3)):
                    across = jnp.sum(jnp.where(diagonal, term, 0.0), axis=0, keepdims=True)
                    extra = jnp.where(line == i, across, extra)
                refs["sg"][z] = jnp.concatenate(tiles + [extra], axis=0).astype(BF16)
                yield from tensor_gather(refs["sg"], g)
                if g == 1:
                    gathers[1].last(0)
                    gathers[1].along(1)
                drain(g)
            else:
                fg, fs = refs["fg"], refs["fs"]
                for t in range(5):
                    fg[z, t] = tiles[t]
                crossing = ids(8)
                refs["crossing"] = crossing

                def hand_across(at):
                    put(crossing + at, fg.at[at, pl.ds(2 - 2 * core, 3)], fs.at[at], sibling)

                yield from tensor_gather(fg, g, hand_across)
                yield

    waiting = [chain(0), chain(1)]
    while waiting:
        for each in list(waiting):
            if next(each, "end") == "end":
                waiting.remove(each)

    def in_order(early, late):
        parts = []
        for j in range(NPR):
            parts += [early[4 * j : 4 * j + 4], late[2 * j : 2 * j + 2]]
        return jnp.concatenate(parts, axis=0)

    for at in range(8):
        for t in range(3):
            both = [buffers[g]["fg"][at, 2 * core + t] for g in range(2)]
            out_rows[my_rows(chip_of(at)), 128 * t : 128 * t + 128] = in_order(*both)
    for at in range(8):
        for g in range(2):
            arrived(buffers[g]["crossing"] + at, buffers[g]["fs"].at[at])
        theirs = pl.ds(pl.multiple_of(chip_of(at) * CHIP + (1 - core) * OWN, 8), OWN)
        for t in range(3):
            both = [buffers[g]["fs"][at, t] for g in range(2)]
            out_rows[theirs, 128 * t : 128 * t + 128] = in_order(*both)
    out_cols[...] = out_rows[...].T
    out_ref[...] = out_cols[pl.ds(pl.multiple_of(core * 64, 8), COLS), :]
    for each in range(3):
        drain(each)


NAMES = (
    "rows", "s0", "s1", "x0relay", "x0dir", "x0fin", "x1relay", "x1dir", "x1fin", "y1r", "y0r",
    "gat", "ob", "d1r", "d2r", "sg", "fg", "fs",
)


def group_scratch(count):
    vmem = pltpu.VMEM
    return [
        vmem((8, count, 2 * COLS), F32),
        vmem((4, 2, count, WIDE0), F32),
        vmem((2, 4, count, PART1), F32),
        *[vmem((LAYERS, 2, count, WIDE0), F32)] * 3,
        *[vmem((LAYERS, count, PART1), F32)] * 3,
        vmem((LAYERS, 4, count, PART1), F32),
        vmem((LAYERS, count, WIDE0), F32),
        vmem((LAYERS, 8, 16, 64 * count), BF16),
        vmem((8, count, 2 * COLS), F32),
        vmem((LAYERS, 4, count, 2 * COLS), F32),
        vmem((LAYERS, 3, count, 2 * COLS), F32),
        vmem((8, 6 * count, 128), BF16),
        vmem((8, 5, count, 128), F32),
        vmem((8, 3, count, 128), F32),
    ]


def on_device(hidden_in, prompt_len, cached_prompt_keys, cached_prompt_values, query_key_value_weight, w_out):
    keys = cached_prompt_keys.reshape(LAYERS, 128, HEAD)
    values = cached_prompt_values.reshape(LAYERS, 128, HEAD)
    half = np.power(ROPE_BASE, -2.0 * np.arange(64) / HEAD)
    freq = jnp.asarray(np.concatenate([half, half])[None, :], F32)
    vmem = pltpu.VMEM
    scratch = [
        vmem((2, COLS, ROWS), F32),
        vmem((ROWS, 2 * COLS), F32),
        vmem((LAYERS, 2, COLS, 1280), BF16),
        vmem((LAYERS, 2, COLS, 1024), BF16),
        vmem((LAYERS, 1024, 2 * COLS), BF16),
        vmem((LAYERS, 128, HEAD), BF16),
        vmem((LAYERS, 17, 2, 128, HEAD), BF16),
        vmem((2, 16, 128), F32),
        vmem((2, 16, 128), F32),
        vmem((2, 128, 128), jnp.int32),
        vmem((2, 128, 128), jnp.int32),
        vmem((16, HEAD), F32),
        vmem((ROWS, PAD), F32),
        vmem((PAD, ROWS), F32),
        *group_scratch(GROUPS[0]),
        *group_scratch(GROUPS[1]),
        pltpu.SemaphoreType.DMA((9,)),
        pltpu.SemaphoreType.DMA((COPIES,)),
        pltpu.SemaphoreType.DMA((COPIES,)),
    ]
    hbm = pl.BlockSpec(memory_space=pl.ANY)
    out = pl.pallas_call(
        kernel,
        out_shape=jax.ShapeDtypeStruct((COLS, ROWS), F32),
        in_specs=[
            pl.BlockSpec(memory_space=pltpu.SMEM),
            pl.BlockSpec(memory_space=pltpu.VMEM),
            hbm, hbm, hbm, hbm, hbm,
        ],
        out_specs=pl.BlockSpec(memory_space=pltpu.VMEM),
        scratch_shapes=scratch,
        compiler_params=pltpu.CompilerParams(
            collective_id=0, has_side_effects=True, vmem_limit_bytes=60 * 1024 * 1024
        ),
        name="two_layers",
    )(prompt_len, freq, hidden_in.T, keys, values, query_key_value_weight, w_out.transpose(0, 2, 1))
    return out.T


def solution(mesh):
    return jax.shard_map(
        on_device,
        mesh=mesh,
        in_specs=(
            P("prompt", "sample"),
            P("prompt"),
            P(None, ("prompt", "sample"), "tensor", None),
            P(None, ("prompt", "sample"), "tensor", None),
            P(None, "sample", "tensor"),
            P(None, "tensor", "sample"),
        ),
        out_specs=P("prompt", "sample"),
        check_vma=False,
    )
```

```python
import jax
import jax.numpy as jnp
import numpy as np
from jax import lax
from jax.experimental import pallas as pl
from jax.experimental.pallas import tpu as pltpu
from jax.sharding import PartitionSpec as P

STEPS = 6
NPR = 4
HEADS = 8
HEAD = 128
LAYERS = 2
ROPE_BASE = 1000000.0
EPSILON = 1e-06
NEGATIVE = -1e30
WIDTH = 5120
ROWS = 384
OWN = 24
CHIP = 48
COLS = 320
PAD = 384
PART0 = 640
PART1 = 640
WIDE0 = PART0 + 128
COPIES = 192
GROUPS = (16, 8)
MESH = pl.DeviceIdType.MESH
F32 = jnp.float32
BF16 = jnp.bfloat16


def dot(a, b):
    return jnp.dot(a, b, preferred_element_type=F32)


def iota(shape, axis):
    return lax.broadcasted_iota(jnp.int32, shape, axis)


def kernel(
    len_ref, freq_ref, hid_hbm, key_hbm, val_hbm, win_hbm, wout_hbm, out_ref,
    hid_across, hid, win, wpad, wout, val, kv, cos_ref, sin_ref, past_ref, length_ref, newest, out_rows, out_cols,
    *grouped,
):
    load_sem, send_sem, recv_sem = grouped[-3:]
    s = lax.axis_index("sample")
    z = lax.axis_index("tensor")
    core = s % 2
    chip = s // 2
    x = chip % 4
    y = chip // 4
    other = 1 - y
    sigma = 1 - 2 * core
    ahead = (x + sigma + 4) % 4
    behind = (x - sigma + 4) % 4
    far = (x + 2) % 4
    delta = 2 * ((z + core) % 2) - 1

    def place(py, px, pc):
        return (py * 4 + px) * 2 + pc

    def ring(step):
        return (z + delta * step + 8) % 8

    def chip_of(at):
        return (at % 2) * 4 + at // 2

    sibling = {"sample": place(y, x, 1 - core)}
    to_ahead = {"sample": place(y, ahead, core)}
    to_behind = {"sample": place(y, behind, core)}
    to_other = {"sample": place(other, x, core)}
    to_other_ahead = {"sample": place(other, ahead, core)}
    to_other_behind = {"sample": place(other, behind, core)}
    partner = {"tensor": ring(-1)}

    used = [0]
    pending = [[], [], []]

    def ids(count):
        first = used[0]
        used[0] += count
        return first

    def send(index, src, dst, device, chain=2):
        copy = pltpu.make_async_remote_copy(
            src_ref=src, dst_ref=dst, send_sem=send_sem.at[index], recv_sem=recv_sem.at[index],
            device_id=device, device_id_type=MESH,
        )
        copy.start()
        pending[chain].append(copy)

    def arrived(index, ref):
        pltpu.make_async_remote_copy(
            src_ref=ref, dst_ref=ref, send_sem=send_sem.at[index], recv_sem=recv_sem.at[index],
            device_id=sibling, device_id_type=MESH,
        ).wait_recv()

    def drain(chain):
        for copy in pending[chain]:
            copy.wait_send()
        pending[chain].clear()

    loads = {}

    def load(name, index, src, dst):
        loads[name] = pltpu.make_async_copy(src, dst, load_sem.at[index])
        loads[name].start()

    load("hid", 0, hid_hbm, hid_across.at[core])
    load(("win", 0), 1, win_hbm.at[0], win.at[0, core])
    for layer in range(LAYERS):
        load(("key", layer), 2 + 2 * layer, key_hbm.at[layer], kv.at[layer, s, 0])
        load(("val", layer), 3 + 2 * layer, val_hbm.at[layer], val.at[layer])
    load(("wout", 0), 6, wout_hbm.at[0], wpad.at[0, core])
    load(("win", 1), 7, win_hbm.at[1], win.at[1, core])
    load(("wout", 1), 8, wout_hbm.at[1], wpad.at[1, core])

    barrier = pltpu.get_barrier_semaphore()
    near = [sibling, to_ahead, to_behind, to_other, to_other_ahead, to_other_behind]
    near += [{"tensor": ring(step)} for step in (-1, 1, 2, -2, 3)]
    for device in near:
        pl.semaphore_signal(barrier, inc=1, device_id=device, device_id_type=MESH)
    pl.semaphore_wait(barrier, len(near))

    shared = ids(6)
    send(shared + 0, hid_hbm, hid_across.at[core], sibling)
    last_half, first_half = pl.ds(PART0, PART1), pl.ds(0, PART0)
    send(shared + 1, win_hbm.at[0, :, last_half], win.at[0, core, :, last_half], sibling)
    send(shared + 5, win_hbm.at[0, :, first_half], win.at[0, core, :, first_half], sibling)

    class Gather:
        def __init__(self, buf):
            self.buf = buf
            self.first = ids(15)

        def put(self, number, py, px, device, pc=None):
            block = self.buf.at[place(py, px, core)]
            send(self.first + number, block, block, device)

        def get(self, number, py, px, pc=None):
            where = place(py, px, core if pc is None else pc)
            arrived(self.first + number, self.buf.at[where])

        def begin(self):
            self.put(0, y, x, to_other)
            self.put(1, y, x, to_ahead)
            self.put(2, y, x, to_behind)
            self.put(7, y, x, sibling)

        def cross(self):
            self.get(0, other, x)
            self.put(4, other, x, to_ahead)
            self.put(5, other, x, to_behind)
            self.put(11, other, x, sibling)

        def along(self, half):
            py, at, near_core = (y, 1, 8) if half == 0 else (other, 4, 12)
            self.get(at, py, behind)
            self.put(at + 2, py, behind, to_ahead)
            self.put(near_core, py, behind, sibling)
            self.get(at + 1, py, ahead)
            self.put(near_core + 1, py, ahead, sibling)

        def last(self, half):
            py, at, near_core = (y, 3, 10) if half == 0 else (other, 6, 14)
            self.get(at, py, far)
            self.put(near_core, py, far, sibling)

        def core_side(self, half):
            py, at = (y, 7) if half == 0 else (other, 11)
            for number, px in enumerate((x, ahead, behind, far)):
                self.get(at + number, py, px, 1 - core)

    gathers = [Gather(kv.at[layer]) for layer in range(LAYERS)]

    def begin_prompt(layer):
        loads[("key", layer)].wait()
        loads[("val", layer)].wait()
        kv[layer, s, 1] = val[layer].astype(F32).T.astype(BF16)
        gathers[layer].begin()

    begin_prompt(0)


    def my_rows(q):
        return pl.ds(pl.multiple_of(q * CHIP + core * OWN, 8), OWN)

    loads["hid"].wait()
    arrived(shared + 0, hid_across.at[1 - core])
    hid[...] = hid_across[...].reshape(2 * COLS, ROWS).T
    buffers = [grouped[len(NAMES) * g : len(NAMES) * g + len(NAMES)] for g in range(2)]
    buffers = [dict(zip(NAMES, refs)) for refs in buffers]
    for q in range(8):
        piece = hid[my_rows(q), :]
        buffers[0]["rows"][q] = jnp.concatenate([piece[6 * j : 6 * j + 4] for j in range(NPR)], axis=0)
        buffers[1]["rows"][q] = jnp.concatenate([piece[6 * j + 4 : 6 * j + 6] for j in range(NPR)], axis=0)

    gathers[0].cross()
    gathers[0].along(0)

    def turn(layer, quarter):
        if quarter == 0:
            loads[("wout", layer)].wait()
            arrived(shared + 2 + 2 * layer, wpad.at[layer, 1 - core])
        part = slice(256 * quarter, 256 * quarter + 256)
        wout[layer, part] = wpad[layer, :, :, part].reshape(2 * COLS, 256).T

    def sample_and_step(row, g):
        sample = lax.shift_right_logical(row, 2 - g)
        return sample, row - sample * (4 - 2 * g) + 4 * g

    def tables(g):
        count = GROUPS[g]
        lane = iota((count, 128), 1)
        sample, step = sample_and_step(iota((count, 128), 0), g)
        length = jnp.zeros((count, 128), jnp.int32)
        for k in range(NPR):
            length = jnp.where(sample == k, len_ref[k], length)
        angle = (length + step).astype(F32) * freq_ref[...]
        cos_ref[g, :count] = jnp.cos(angle)
        sin_ref[g, :count] = jnp.where(lane < 64, -jnp.sin(angle), jnp.sin(angle))
        key = iota((128, 128), 0)
        query = iota((128, 128), 1)
        sample, _ = sample_and_step(query % count, g)
        length = jnp.zeros((128, 128), jnp.int32)
        start = jnp.zeros((128, 128), jnp.int32)
        offset = jnp.int32(0)
        for k in range(NPR):
            length = jnp.where(sample == k, len_ref[k], length)
            start = jnp.where(sample == k, offset, start)
            offset = offset + len_ref[k]
        past_ref[g] = key - start
        length_ref[g] = length

    def recent(g):
        key = iota((128, 128), 0)
        sample, step = sample_and_step(iota((128, 128), 1) % GROUPS[g], g)
        early_sample, early_step = sample_and_step(key, 0)
        late_sample, late_step = sample_and_step(key - 16, 1)
        seen = (key < 16) & (early_sample == sample) & (early_step <= step)
        return seen | ((key >= 16) & (key < 24) & (late_sample == sample) & (late_step <= step))

    def attend(layer, g, part0, part1):
        count = GROUPS[g]
        inverse = lax.rsqrt(part0[:, PART0:] / WIDTH + EPSILON)
        cosine = cos_ref[g, :count]
        sine = sin_ref[g, :count]

        def rotate(vector):
            return vector * cosine + pltpu.roll(vector, 64, 1) * sine

        blocks = [part0[:, HEAD * h : HEAD * h + HEAD] * inverse for h in range(5)]
        blocks += [part1[:, HEAD * h : HEAD * h + HEAD] * inverse for h in range(5)]
        queries = [rotate(block) * HEAD**-0.5 for block in blocks[:HEADS]]
        if g == 1:
            queries.append(jnp.zeros((64, HEAD), F32))
        queries = jnp.concatenate(queries, axis=0).T
        first = queries.astype(BF16)
        rest = queries - first.astype(F32)
        second = rest.astype(BF16)
        third = (rest - second.astype(F32)).astype(BF16)
        upper = jnp.concatenate([first, second], axis=0)
        if g == 0:
            newest[...] = blocks[9]
            empty = jnp.zeros((112, HEAD), F32)
            kv[layer, 16, 0] = jnp.concatenate([rotate(blocks[8]), empty], axis=0).astype(BF16)
            kv[layer, 16, 1] = jnp.concatenate([blocks[9], empty], axis=0).T.astype(BF16)
        else:
            empty = jnp.zeros((8, HEAD), F32)
            kv[layer, 16, 0, 16:32] = jnp.concatenate([rotate(blocks[8]), empty], axis=0).astype(BF16)
            empty = jnp.zeros((104, HEAD), F32)
            kv[layer, 16, 1] = jnp.concatenate([newest[...], blocks[9], empty], axis=0).T.astype(BF16)

        def visit(block, count, seen, running):
            peak, total, summed = running
            keys = kv[layer, pl.ds(block, count), 0].reshape(count * 128, HEAD)
            scores = dot(keys, third) + dot(jnp.concatenate([keys, keys], axis=1), upper)
            parts = []
            for i in range(count):
                part = scores[128 * i : 128 * i + 128] + jnp.where(seen(i), 0.0, NEGATIVE)
                maxima = jnp.max(part, axis=0, keepdims=True)
                weights = jnp.exp(part - maxima)
                sums = jnp.sum(weights, axis=0, keepdims=True)
                parts.append((maxima, sums, dot(kv[layer, block + i, 1], weights.astype(BF16))))
            higher = peak
            for maxima, _, _ in parts:
                higher = jnp.maximum(higher, maxima)
            left = jnp.exp(peak - higher)
            total = total * left
            summed = summed * left
            for maxima, sums, values in parts:
                right = jnp.exp(maxima - higher)
                total = total + sums * right
                summed = summed + values * right
            return higher, total, summed

        running = (jnp.full((1, 128), NEGATIVE, F32), jnp.zeros((1, 128), F32), jnp.zeros((HEAD, 128), F32))
        running = visit(16, 1, lambda i: recent(g), running)

        def prompt_blocks(group, running):
            def seen(i):
                past = past_ref[g] + (group * 4 + i) * 128
                return (past >= 0) & (past < length_ref[g])

            return visit(group * 4, 4, seen, running)

        _, total, summed = lax.fori_loop(0, 4, prompt_blocks, running)
        rows = (summed / total).T
        heads = [rows[count * h : count * h + count] for h in range(HEADS)]
        if g == 0:
            return jnp.concatenate(heads, axis=1).astype(BF16)
        halves = [jnp.concatenate(heads[:4], axis=1), jnp.concatenate(heads[4:], axis=1)]
        return jnp.concatenate(halves, axis=0).astype(BF16)

    def tensor_gather(buf, chain, held=lambda at: None):
        first = ids(7)
        mine = buf.at[z]
        send(first + 2, mine, mine, {"tensor": ring(3)}, chain)
        send(first + 1, mine, mine, {"tensor": ring(-2)}, chain)
        send(first + 0, mine, mine, {"tensor": ring(1)}, chain)
        send(first + 3, mine, mine, partner, chain)
        held(z)
        yield
        for k in (1, 2, 3):
            block = buf.at[ring(k)]
            arrived(first + k - 1, block)
            send(first + 3 + k, block, block, partner, chain)
            held(ring(k))
        yield
        for k in (0, 1, 2, 3):
            arrived(first + 3 + k, buf.at[ring(-1 - k)])
            held(ring(-1 - k))

    def chain(g):
        count = GROUPS[g]
        refs = buffers[g]
        s0, s1, own = refs["s0"], refs["s1"], refs["rows"]
        gat, ob = refs["gat"], refs["ob"]
        diagonal = iota((count, 128), 0) == iota((count, 128), 1)

        def put(index, src, dst, device):
            send(index, src, dst, device, g)

        for layer in range(LAYERS):
            pieces = []
            for q in range(8):
                if layer == 0:
                    piece = own[q]
                    squares = jnp.sum(piece * piece, axis=1, keepdims=True)
                else:
                    block = refs["sg"][2 * (q % 4) + q // 4].astype(F32)
                    across = jnp.sum(block[5 * count :], axis=0, keepdims=True)
                    squares = jnp.sum(jnp.where(diagonal, across, 0.0), axis=1, keepdims=True)
                    piece = jnp.concatenate([block[count * t : count * t + count] for t in range(5)], axis=1)
                s0[q % 4, q // 4, :, PART0:] = jnp.broadcast_to(squares, (count, 128))
                pieces.append(piece)
            rows = jnp.concatenate(pieces, axis=0).astype(BF16)

            first = ids(14)
            if g == 0:
                loads[("win", layer)].wait()
                if layer == 0:
                    arrived(shared + 1, win.at[0, 1 - core, :, last_half])
                else:
                    arrived(shared + 3, win.at[1, 1 - core])
            x0relay, x0dir, x0fin = (refs[name].at[layer] for name in ("x0relay", "x0dir", "x0fin"))
            x1relay, x1dir, x1fin = (refs[name].at[layer] for name in ("x1relay", "x1dir", "x1fin"))
            y1r, y0r = refs["y1r"].at[layer], refs["y0r"].at[layer]
            part = dot(rows, win[layer, :, :, PART0:].reshape(2 * COLS, PART1))
            s1[...] = part.reshape(2, 4, count, PART1)
            for number, px in enumerate((far, behind, ahead, x)):
                put(first + number, s1.at[other, px], y1r.at[px], to_other)
            if g == 0 and layer == 0:
                arrived(shared + 5, win.at[0, 1 - core, :, first_half])
            part = dot(rows, win[layer, :, :, :PART0].reshape(2 * COLS, PART0))
            for q in range(8):
                s0[q % 4, q // 4, :, :PART0] = part[count * q : count * q + count]
            for number, py in enumerate((other, y)):
                put(first + 4 + number, s0.at[far, py], x0relay.at[py], to_ahead)
                put(first + 6 + number, s0.at[behind, py], x0dir.at[py], to_behind)
            if g == 1 and layer == 0:
                tables(0)
                tables(1)
            elif g == 1:
                turn(1, 0)
            yield
            if g == 0 and layer == 0:
                gathers[0].last(0)
                gathers[0].along(1)

            def pass_on(number, py):
                arrived(first + 4 + number, x0relay.at[py])
                s0[ahead, py] = s0[ahead, py] + x0relay[py]
                put(first + 8 + number, s0.at[ahead, py], x0fin.at[py], to_ahead)

            pass_on(0, other)
            for number, px, to, device in ((0, far, x1relay, to_ahead), (1, behind, x1dir, to_behind)):
                arrived(first + number, y1r.at[px])
                s1[y, px] = s1[y, px] + y1r[px]
                put(first + 10 + number, s1.at[y, px], to, device)
            pass_on(1, y)
            if g == 1 and layer == 1:
                turn(1, 1)
                turn(1, 2)
            yield
            if g == 0 and layer == 0:
                gathers[0].last(1)
                send(shared + 2, wout_hbm.at[0], wpad.at[0, core], sibling)
            arrived(first + 6, x0dir.at[other])
            arrived(first + 8, x0fin.at[other])
            s0[x, other] = s0[x, other] + x0dir[other] + x0fin[other]
            put(first + 13, s0.at[x, other], y0r, to_other)
            arrived(first + 10, x1relay)
            arrived(first + 2, y1r.at[ahead])
            s1[y, ahead] = s1[y, ahead] + y1r[ahead] + x1relay[...]
            put(first + 12, s1.at[y, ahead], x1fin, to_ahead)
            if g == 1 and layer == 1:
                turn(1, 3)
            yield
            if g == 0:
                if layer == 1:
                    gathers[1].last(1)
                gathers[layer].core_side(0)
                gathers[layer].core_side(1)
            arrived(first + 3, y1r.at[x])
            arrived(first + 11, x1dir)
            arrived(first + 12, x1fin)
            part1 = s1[y, x] + y1r[x] + x1dir[...] + x1fin[...]
            arrived(first + 7, x0dir.at[y])
            arrived(first + 9, x0fin.at[y])
            part0 = s0[x, y] + x0dir[y] + x0fin[y]
            arrived(first + 13, y0r)
            part0 = part0 + y0r[...]
            gat[layer, chip] = attend(layer, g, part0, part1)

            first = ids(7)
            mine = gat.at[layer, chip]
            put(first + 0, mine, mine, to_ahead)
            put(first + 1, mine, mine, to_behind)
            put(first + 3, mine, mine, to_other_ahead)
            put(first + 4, mine, mine, to_other_behind)
            put(first + 2, mine, mine, to_other)
            if g == 1 and layer == 0:
                send(shared + 3, win_hbm.at[1], win.at[1, core], sibling)
                turn(0, 0)
                turn(0, 1)
            yield
            places = ((0, y, behind), (3, other, behind), (1, y, ahead), (2, other, x), (4, other, ahead))
            places += ((5, y, far), (6, other, far))
            for number, py, px in places[:2]:
                block = gat.at[layer, py * 4 + px]
                arrived(first + number, block)
                put(first + (5 if number == 0 else 6), block, block, to_ahead)
            if g == 1 and layer == 0:
                turn(0, 2)
                turn(0, 3)
            yield
            for number, py, px in places[2:]:
                arrived(first + number, gat.at[layer, py * 4 + px])
            if g == 0:
                rows = gat[layer].reshape(8 * count, 1024)
            else:
                blocks = gat[layer].astype(F32)
                rows = [jnp.concatenate([blocks[q, :count], blocks[q, count:]], axis=1) for q in range(8)]
                rows = jnp.concatenate(rows, axis=0).astype(BF16)
            ob[...] = dot(rows, wout[layer]).reshape(8, count, 2 * COLS)

            first = ids(7)
            d1r, d2r = refs["d1r"], refs["d2r"]
            for k in (3, 2, 1, 0):
                put(first + k, ob.at[chip_of(ring(-1 - k))], d1r.at[layer, k], partner)
            if layer == 0 and g == 1:
                begin_prompt(1)
            yield
            for k in (3, 2, 1):
                at = ring(k)
                block = ob.at[chip_of(at)]
                arrived(first + k, d1r.at[layer, k])
                block[...] = block[...] + d1r[layer, k]
                put(first + 3 + k, block, d2r.at[layer, k - 1], {"tensor": at})
            arrived(first + 0, d1r.at[layer, 0])
            stream = own[chip_of(z)] + ob[chip_of(z)] + d1r[layer, 0]
            if layer == 0 and g == 1:
                gathers[1].cross()
                gathers[1].along(0)
            yield
            for k in (1, 2, 3):
                arrived(first + 3 + k, d2r.at[layer, k - 1])
                stream = stream + d2r[layer, k - 1]
            tiles = [stream[:, 128 * t : 128 * t + 128] for t in range(5)]
            if layer == 0:
                own[chip_of(z)] = stream
                squares = jnp.sum(stream * stream, axis=1, keepdims=True)
                square1 = squares.astype(BF16).astype(F32)
                square2 = (squares - square1).astype(BF16).astype(F32)
                square3 = squares - square1 - square2
                line = iota((count, 128), 0)
                extra = jnp.zeros((count, 128), F32)
                for i, term in enumerate((square1, square2, square3)):
                    across = jnp.sum(jnp.where(diagonal, term, 0.0), axis=0, keepdims=True)
                    extra = jnp.where(line == i, across, extra)
                refs["sg"][z] = jnp.concatenate(tiles + [extra], axis=0).astype(BF16)
                yield from tensor_gather(refs["sg"], g)
                if g == 1:
                    gathers[1].last(0)
                    gathers[1].along(1)
                    send(shared + 4, wout_hbm.at[1], wpad.at[1, core], sibling)
                drain(g)
            else:
                fg, fs = refs["fg"], refs["fs"]
                for t in range(5):
                    fg[z, t] = tiles[t]
                crossing = ids(8)
                refs["crossing"] = crossing

                def hand_across(at):
                    put(crossing + at, fg.at[at, pl.ds(2 - 2 * core, 3)], fs.at[at], sibling)

                yield from tensor_gather(fg, g, hand_across)
                yield

    waiting = [chain(0), chain(1)]
    while waiting:
        for each in list(waiting):
            if next(each, "end") == "end":
                waiting.remove(each)

    def in_order(early, late):
        parts = []
        for j in range(NPR):
            parts += [early[4 * j : 4 * j + 4], late[2 * j : 2 * j + 2]]
        return jnp.concatenate(parts, axis=0)

    for at in range(8):
        for t in range(3):
            both = [buffers[g]["fg"][at, 2 * core + t] for g in range(2)]
            out_rows[my_rows(chip_of(at)), 128 * t : 128 * t + 128] = in_order(*both)
    for at in range(8):
        for g in range(2):
            arrived(buffers[g]["crossing"] + at, buffers[g]["fs"].at[at])
        theirs = pl.ds(pl.multiple_of(chip_of(at) * CHIP + (1 - core) * OWN, 8), OWN)
        for t in range(3):
            both = [buffers[g]["fs"][at, t] for g in range(2)]
            out_rows[theirs, 128 * t : 128 * t + 128] = in_order(*both)
    out_cols[...] = out_rows[...].T
    out_ref[...] = out_cols[pl.ds(pl.multiple_of(core * 64, 8), COLS), :]
    for each in range(3):
        drain(each)


NAMES = (
    "rows", "s0", "s1", "x0relay", "x0dir", "x0fin", "x1relay", "x1dir", "x1fin", "y1r", "y0r",
    "gat", "ob", "d1r", "d2r", "sg", "fg", "fs",
)


def group_scratch(count):
    vmem = pltpu.VMEM
    return [
        vmem((8, count, 2 * COLS), F32),
        vmem((4, 2, count, WIDE0), F32),
        vmem((2, 4, count, PART1), F32),
        *[vmem((LAYERS, 2, count, WIDE0), F32)] * 3,
        *[vmem((LAYERS, count, PART1), F32)] * 3,
        vmem((LAYERS, 4, count, PART1), F32),
        vmem((LAYERS, count, WIDE0), F32),
        vmem((LAYERS, 8, 16, 64 * count), BF16),
        vmem((8, count, 2 * COLS), F32),
        vmem((LAYERS, 4, count, 2 * COLS), F32),
        vmem((LAYERS, 3, count, 2 * COLS), F32),
        vmem((8, 6 * count, 128), BF16),
        vmem((8, 5, count, 128), F32),
        vmem((8, 3, count, 128), F32),
    ]


def on_device(hidden_in, prompt_len, cached_prompt_keys, cached_prompt_values, query_key_value_weight, w_out):
    keys = cached_prompt_keys.reshape(LAYERS, 128, HEAD)
    values = cached_prompt_values.reshape(LAYERS, 128, HEAD)
    half = np.power(ROPE_BASE, -2.0 * np.arange(64) / HEAD)
    freq = jnp.asarray(np.concatenate([half, half])[None, :], F32)
    vmem = pltpu.VMEM
    scratch = [
        vmem((2, COLS, ROWS), F32),
        vmem((ROWS, 2 * COLS), F32),
        vmem((LAYERS, 2, COLS, 1280), BF16),
        vmem((LAYERS, 2, COLS, 1024), BF16),
        vmem((LAYERS, 1024, 2 * COLS), BF16),
        vmem((LAYERS, 128, HEAD), BF16),
        vmem((LAYERS, 17, 2, 128, HEAD), BF16),
        vmem((2, 16, 128), F32),
        vmem((2, 16, 128), F32),
        vmem((2, 128, 128), jnp.int32),
        vmem((2, 128, 128), jnp.int32),
        vmem((16, HEAD), F32),
        vmem((ROWS, PAD), F32),
        vmem((PAD, ROWS), F32),
        *group_scratch(GROUPS[0]),
        *group_scratch(GROUPS[1]),
        pltpu.SemaphoreType.DMA((9,)),
        pltpu.SemaphoreType.DMA((COPIES,)),
        pltpu.SemaphoreType.DMA((COPIES,)),
    ]
    hbm = pl.BlockSpec(memory_space=pl.ANY)
    out = pl.pallas_call(
        kernel,
        out_shape=jax.ShapeDtypeStruct((COLS, ROWS), F32),
        in_specs=[
            pl.BlockSpec(memory_space=pltpu.SMEM),
            pl.BlockSpec(memory_space=pltpu.VMEM),
            hbm, hbm, hbm, hbm, hbm,
        ],
        out_specs=pl.BlockSpec(memory_space=pltpu.VMEM),
        scratch_shapes=scratch,
        compiler_params=pltpu.CompilerParams(
            collective_id=0, has_side_effects=True, vmem_limit_bytes=60 * 1024 * 1024
        ),
        name="two_layers",
    )(prompt_len, freq, hidden_in.T, keys, values, query_key_value_weight, w_out.transpose(0, 2, 1))
    return out.T


def solution(mesh):
    return jax.shard_map(
        on_device,
        mesh=mesh,
        in_specs=(
            P("prompt", "sample"),
            P("prompt"),
            P(None, ("prompt", "sample"), "tensor", None),
            P(None, ("prompt", "sample"), "tensor", None),
            P(None, "sample", "tensor"),
            P(None, "tensor", "sample"),
        ),
        out_specs=P("prompt", "sample"),
        check_vma=False,
    )
```

```python
import jax
import jax.numpy as jnp
import numpy as np
from jax import lax
from jax.experimental import pallas as pl
from jax.experimental.pallas import tpu as pltpu
from jax.sharding import PartitionSpec as P

STEPS = 6
NPR = 4
HEADS = 8
HEAD = 128
LAYERS = 2
ROPE_BASE = 1000000.0
EPSILON = 1e-06
NEGATIVE = -1e30
WIDTH = 5120
ROWS = 384
OWN = 24
CHIP = 48
COLS = 320
PAD = 384
PART0 = 640
PART1 = 640
WIDE0 = PART0 + 128
COPIES = 192
GROUPS = (16, 8)
MESH = pl.DeviceIdType.MESH
F32 = jnp.float32
BF16 = jnp.bfloat16


def dot(a, b):
    return jnp.dot(a, b, preferred_element_type=F32)


def iota(shape, axis):
    return lax.broadcasted_iota(jnp.int32, shape, axis)


def kernel(
    len_ref, freq_ref, hid_hbm, key_hbm, val_hbm, win_hbm, wout_hbm, out_ref,
    hid_across, hid, win, wpad, wout, val, kv, cos_ref, sin_ref, past_ref, length_ref, newest, out_rows, out_cols,
    *grouped,
):
    load_sem, send_sem, recv_sem = grouped[-3:]
    s = lax.axis_index("sample")
    z = lax.axis_index("tensor")
    core = s % 2
    chip = s // 2
    x = chip % 4
    y = chip // 4
    other = 1 - y
    sigma = 1 - 2 * core
    ahead = (x + sigma + 4) % 4
    behind = (x - sigma + 4) % 4
    far = (x + 2) % 4
    delta = 2 * ((z + core) % 2) - 1

    def place(py, px, pc):
        return (py * 4 + px) * 2 + pc

    def ring(step):
        return (z + delta * step + 8) % 8

    def chip_of(at):
        return (at % 2) * 4 + at // 2

    sibling = {"sample": place(y, x, 1 - core)}
    to_ahead = {"sample": place(y, ahead, core)}
    to_behind = {"sample": place(y, behind, core)}
    to_other = {"sample": place(other, x, core)}
    to_other_ahead = {"sample": place(other, ahead, core)}
    to_other_behind = {"sample": place(other, behind, core)}
    partner = {"tensor": ring(-1)}

    used = [0]
    pending = [[], [], []]

    def ids(count):
        first = used[0]
        used[0] += count
        return first

    def send(index, src, dst, device, chain=2):
        copy = pltpu.make_async_remote_copy(
            src_ref=src, dst_ref=dst, send_sem=send_sem.at[index], recv_sem=recv_sem.at[index],
            device_id=device, device_id_type=MESH,
        )
        copy.start()
        pending[chain].append(copy)

    def arrived(index, ref):
        pltpu.make_async_remote_copy(
            src_ref=ref, dst_ref=ref, send_sem=send_sem.at[index], recv_sem=recv_sem.at[index],
            device_id=sibling, device_id_type=MESH,
        ).wait_recv()

    def drain(chain):
        for copy in pending[chain]:
            copy.wait_send()
        pending[chain].clear()

    loads = {}

    def load(name, index, src, dst):
        loads[name] = pltpu.make_async_copy(src, dst, load_sem.at[index])
        loads[name].start()

    load("hid", 0, hid_hbm, hid_across.at[core])
    load(("win", 0), 1, win_hbm.at[0], win.at[0, core])
    for layer in range(LAYERS):
        load(("key", layer), 2 + 2 * layer, key_hbm.at[layer], kv.at[layer, s, 0])
        load(("val", layer), 3 + 2 * layer, val_hbm.at[layer], val.at[layer])
    load(("wout", 0), 6, wout_hbm.at[0], wpad.at[0, core])
    load(("win", 1), 7, win_hbm.at[1], win.at[1, core])
    load(("wout", 1), 8, wout_hbm.at[1], wpad.at[1, core])

    barrier = pltpu.get_barrier_semaphore()
    near = [sibling, to_ahead, to_behind, to_other, to_other_ahead, to_other_behind]
    near += [{"tensor": ring(step)} for step in (-1, 1, 2, -2, 3)]
    for device in near:
        pl.semaphore_signal(barrier, inc=1, device_id=device, device_id_type=MESH)
    pl.semaphore_wait(barrier, len(near))

    shared = ids(6)
    send(shared + 0, hid_hbm, hid_across.at[core], sibling)
    last_half, first_half = pl.ds(PART0, PART1), pl.ds(0, PART0)
    send(shared + 1, win_hbm.at[0, :, last_half], win.at[0, core, :, last_half], sibling)
    send(shared + 5, win_hbm.at[0, :, first_half], win.at[0, core, :, first_half], sibling)

    class Gather:
        def __init__(self, buf):
            self.buf = buf
            self.first = ids(15)

        def put(self, number, py, px, device, pc=None):
            block = self.buf.at[place(py, px, core)]
            send(self.first + number, block, block, device)

        def get(self, number, py, px, pc=None):
            where = place(py, px, core if pc is None else pc)
            arrived(self.first + number, self.buf.at[where])

        def begin(self):
            self.put(0, y, x, to_other)
            self.put(1, y, x, to_ahead)
            self.put(2, y, x, to_behind)
            self.put(7, y, x, sibling)

        def cross(self):
            self.get(0, other, x)
            self.put(4, other, x, to_ahead)
            self.put(5, other, x, to_behind)
            self.put(11, other, x, sibling)

        def along(self, half):
            py, at, near_core = (y, 1, 8) if half == 0 else (other, 4, 12)
            self.get(at, py, behind)
            self.put(at + 2, py, behind, to_ahead)
            self.put(near_core, py, behind, sibling)
            self.get(at + 1, py, ahead)
            self.put(near_core + 1, py, ahead, sibling)

        def last(self, half):
            py, at, near_core = (y, 3, 10) if half == 0 else (other, 6, 14)
            self.get(at, py, far)
            self.put(near_core, py, far, sibling)

        def core_side(self, half):
            py, at = (y, 7) if half == 0 else (other, 11)
            for number, px in enumerate((x, ahead, behind, far)):
                self.get(at + number, py, px, 1 - core)

    gathers = [Gather(kv.at[layer]) for layer in range(LAYERS)]

    def begin_prompt(layer):
        loads[("key", layer)].wait()
        loads[("val", layer)].wait()
        kv[layer, s, 1] = val[layer].astype(F32).T.astype(BF16)
        gathers[layer].begin()

    begin_prompt(0)

    send(shared + 2, wout_hbm.at[0], wpad.at[0, core], sibling)
    send(shared + 3, win_hbm.at[1], win.at[1, core], sibling)
    send(shared + 4, wout_hbm.at[1], wpad.at[1, core], sibling)

    def my_rows(q):
        return pl.ds(pl.multiple_of(q * CHIP + core * OWN, 8), OWN)

    loads["hid"].wait()
    arrived(shared + 0, hid_across.at[1 - core])
    hid[...] = hid_across[...].reshape(2 * COLS, ROWS).T
    buffers = [grouped[len(NAMES) * g : len(NAMES) * g + len(NAMES)] for g in range(2)]
    buffers = [dict(zip(NAMES, refs)) for refs in buffers]
    for q in range(8):
        piece = hid[my_rows(q), :]
        buffers[0]["rows"][q] = jnp.concatenate([piece[6 * j : 6 * j + 4] for j in range(NPR)], axis=0)
        buffers[1]["rows"][q] = jnp.concatenate([piece[6 * j + 4 : 6 * j + 6] for j in range(NPR)], axis=0)

    gathers[0].cross()
    gathers[0].along(0)

    def turn(layer, quarter):
        if quarter == 0:
            loads[("wout", layer)].wait()
            arrived(shared + 2 + 2 * layer, wpad.at[layer, 1 - core])
        part = slice(256 * quarter, 256 * quarter + 256)
        wout[layer, part] = wpad[layer, :, :, part].reshape(2 * COLS, 256).T

    def sample_and_step(row, g):
        sample = lax.shift_right_logical(row, 2 - g)
        return sample, row - sample * (4 - 2 * g) + 4 * g

    def tables(g):
        count = GROUPS[g]
        lane = iota((count, 128), 1)
        sample, step = sample_and_step(iota((count, 128), 0), g)
        length = jnp.zeros((count, 128), jnp.int32)
        for k in range(NPR):
            length = jnp.where(sample == k, len_ref[k], length)
        angle = (length + step).astype(F32) * freq_ref[...]
        cos_ref[g, :count] = jnp.cos(angle)
        sin_ref[g, :count] = jnp.where(lane < 64, -jnp.sin(angle), jnp.sin(angle))
        key = iota((128, 128), 0)
        query = iota((128, 128), 1)
        sample, _ = sample_and_step(query % count, g)
        length = jnp.zeros((128, 128), jnp.int32)
        start = jnp.zeros((128, 128), jnp.int32)
        offset = jnp.int32(0)
        for k in range(NPR):
            length = jnp.where(sample == k, len_ref[k], length)
            start = jnp.where(sample == k, offset, start)
            offset = offset + len_ref[k]
        past_ref[g] = key - start
        length_ref[g] = length

    def recent(g):
        key = iota((128, 128), 0)
        sample, step = sample_and_step(iota((128, 128), 1) % GROUPS[g], g)
        early_sample, early_step = sample_and_step(key, 0)
        late_sample, late_step = sample_and_step(key - 16, 1)
        seen = (key < 16) & (early_sample == sample) & (early_step <= step)
        return seen | ((key >= 16) & (key < 24) & (late_sample == sample) & (late_step <= step))

    def attend(layer, g, part0, part1):
        count = GROUPS[g]
        inverse = lax.rsqrt(part0[:, PART0:] / WIDTH + EPSILON)
        cosine = cos_ref[g, :count]
        sine = sin_ref[g, :count]

        def rotate(vector):
            return vector * cosine + pltpu.roll(vector, 64, 1) * sine

        blocks = [part0[:, HEAD * h : HEAD * h + HEAD] * inverse for h in range(5)]
        blocks += [part1[:, HEAD * h : HEAD * h + HEAD] * inverse for h in range(5)]
        queries = [rotate(block) * HEAD**-0.5 for block in blocks[:HEADS]]
        if g == 1:
            queries.append(jnp.zeros((64, HEAD), F32))
        queries = jnp.concatenate(queries, axis=0).T
        first = queries.astype(BF16)
        rest = queries - first.astype(F32)
        second = rest.astype(BF16)
        third = (rest - second.astype(F32)).astype(BF16)
        upper = jnp.concatenate([first, second], axis=0)
        if g == 0:
            newest[...] = blocks[9]
            empty = jnp.zeros((112, HEAD), F32)
            kv[layer, 16, 0] = jnp.concatenate([rotate(blocks[8]), empty], axis=0).astype(BF16)
            kv[layer, 16, 1] = jnp.concatenate([blocks[9], empty], axis=0).T.astype(BF16)
        else:
            empty = jnp.zeros((8, HEAD), F32)
            kv[layer, 16, 0, 16:32] = jnp.concatenate([rotate(blocks[8]), empty], axis=0).astype(BF16)
            empty = jnp.zeros((104, HEAD), F32)
            kv[layer, 16, 1] = jnp.concatenate([newest[...], blocks[9], empty], axis=0).T.astype(BF16)

        def visit(block, count, seen, running):
            peak, total, summed = running
            keys = kv[layer, pl.ds(block, count), 0].reshape(count * 128, HEAD)
            scores = dot(keys, third) + dot(jnp.concatenate([keys, keys], axis=1), upper)
            parts = []
            for i in range(count):
                part = scores[128 * i : 128 * i + 128] + jnp.where(seen(i), 0.0, NEGATIVE)
                maxima = jnp.max(part, axis=0, keepdims=True)
                weights = jnp.exp(part - maxima)
                sums = jnp.sum(weights, axis=0, keepdims=True)
                parts.append((maxima, sums, dot(kv[layer, block + i, 1], weights.astype(BF16))))
            higher = peak
            for maxima, _, _ in parts:
                higher = jnp.maximum(higher, maxima)
            left = jnp.exp(peak - higher)
            total = total * left
            summed = summed * left
            for maxima, sums, values in parts:
                right = jnp.exp(maxima - higher)
                total = total + sums * right
                summed = summed + values * right
            return higher, total, summed

        running = (jnp.full((1, 128), NEGATIVE, F32), jnp.zeros((1, 128), F32), jnp.zeros((HEAD, 128), F32))
        running = visit(16, 1, lambda i: recent(g), running)

        def prompt_blocks(group, running):
            def seen(i):
                past = past_ref[g] + (group * 4 + i) * 128
                return (past >= 0) & (past < length_ref[g])

            return visit(group * 4, 4, seen, running)

        _, total, summed = lax.fori_loop(0, 4, prompt_blocks, running, unroll=4)
        rows = (summed / total).T
        heads = [rows[count * h : count * h + count] for h in range(HEADS)]
        if g == 0:
            return jnp.concatenate(heads, axis=1).astype(BF16)
        halves = [jnp.concatenate(heads[:4], axis=1), jnp.concatenate(heads[4:], axis=1)]
        return jnp.concatenate(halves, axis=0).astype(BF16)

    def tensor_gather(buf, chain, held=lambda at: None):
        first = ids(7)
        mine = buf.at[z]
        send(first + 2, mine, mine, {"tensor": ring(3)}, chain)
        send(first + 1, mine, mine, {"tensor": ring(-2)}, chain)
        send(first + 0, mine, mine, {"tensor": ring(1)}, chain)
        send(first + 3, mine, mine, partner, chain)
        held(z)
        yield
        for k in (1, 2, 3):
            block = buf.at[ring(k)]
            arrived(first + k - 1, block)
            send(first + 3 + k, block, block, partner, chain)
            held(ring(k))
        yield
        for k in (0, 1, 2, 3):
            arrived(first + 3 + k, buf.at[ring(-1 - k)])
            held(ring(-1 - k))

    def chain(g):
        count = GROUPS[g]
        refs = buffers[g]
        s0, s1, own = refs["s0"], refs["s1"], refs["rows"]
        gat, ob = refs["gat"], refs["ob"]
        diagonal = iota((count, 128), 0) == iota((count, 128), 1)

        def put(index, src, dst, device):
            send(index, src, dst, device, g)

        for layer in range(LAYERS):
            pieces = []
            for q in range(8):
                if layer == 0:
                    piece = own[q]
                    squares = jnp.sum(piece * piece, axis=1, keepdims=True)
                else:
                    block = refs["sg"][2 * (q % 4) + q // 4].astype(F32)
                    across = jnp.sum(block[5 * count :], axis=0, keepdims=True)
                    squares = jnp.sum(jnp.where(diagonal, across, 0.0), axis=1, keepdims=True)
                    piece = jnp.concatenate([block[count * t : count * t + count] for t in range(5)], axis=1)
                s0[q % 4, q // 4, :, PART0:] = jnp.broadcast_to(squares, (count, 128))
                pieces.append(piece)
            rows = jnp.concatenate(pieces, axis=0).astype(BF16)

            first = ids(14)
            if g == 0:
                loads[("win", layer)].wait()
                if layer == 0:
                    arrived(shared + 1, win.at[0, 1 - core, :, last_half])
                else:
                    arrived(shared + 3, win.at[1, 1 - core])
            x0relay, x0dir, x0fin = (refs[name].at[layer] for name in ("x0relay", "x0dir", "x0fin"))
            x1relay, x1dir, x1fin = (refs[name].at[layer] for name in ("x1relay", "x1dir", "x1fin"))
            y1r, y0r = refs["y1r"].at[layer], refs["y0r"].at[layer]
            part = dot(rows, win[layer, :, :, PART0:].reshape(2 * COLS, PART1))
            s1[...] = part.reshape(2, 4, count, PART1)
            for number, px in enumerate((far, behind, ahead, x)):
                put(first + number, s1.at[other, px], y1r.at[px], to_other)
            if g == 0 and layer == 0:
                arrived(shared + 5, win.at[0, 1 - core, :, first_half])
            part = dot(rows, win[layer, :, :, :PART0].reshape(2 * COLS, PART0))
            for q in range(8):
                s0[q % 4, q // 4, :, :PART0] = part[count * q : count * q + count]
            for number, py in enumerate((other, y)):
                put(first + 4 + number, s0.at[far, py], x0relay.at[py], to_ahead)
                put(first + 6 + number, s0.at[behind, py], x0dir.at[py], to_behind)
            if g == 1 and layer == 0:
                tables(0)
                tables(1)
                turn(0, 0)
            elif g == 1:
                turn(1, 2)
            yield
            if g == 0 and layer == 0:
                gathers[0].last(0)
                gathers[0].along(1)

            def pass_on(number, py):
                arrived(first + 4 + number, x0relay.at[py])
                s0[ahead, py] = s0[ahead, py] + x0relay[py]
                put(first + 8 + number, s0.at[ahead, py], x0fin.at[py], to_ahead)

            pass_on(0, other)
            for number, px, to, device in ((0, far, x1relay, to_ahead), (1, behind, x1dir, to_behind)):
                arrived(first + number, y1r.at[px])
                s1[y, px] = s1[y, px] + y1r[px]
                put(first + 10 + number, s1.at[y, px], to, device)
            pass_on(1, y)
            if g == 1 and layer == 0:
                turn(0, 1)
                turn(0, 2)
            elif g == 1:
                turn(1, 3)
            yield
            if g == 0 and layer == 0:
                gathers[0].last(1)
            arrived(first + 6, x0dir.at[other])
            arrived(first + 8, x0fin.at[other])
            s0[x, other] = s0[x, other] + x0dir[other] + x0fin[other]
            put(first + 13, s0.at[x, other], y0r, to_other)
            arrived(first + 10, x1relay)
            arrived(first + 2, y1r.at[ahead])
            s1[y, ahead] = s1[y, ahead] + y1r[ahead] + x1relay[...]
            put(first + 12, s1.at[y, ahead], x1fin, to_ahead)
            if g == 1 and layer == 0:
                turn(0, 3)
            yield
            if g == 0:
                if layer == 1:
                    gathers[1].last(1)
                gathers[layer].core_side(0)
                gathers[layer].core_side(1)
            arrived(first + 3, y1r.at[x])
            arrived(first + 11, x1dir)
            arrived(first + 12, x1fin)
            part1 = s1[y, x] + y1r[x] + x1dir[...] + x1fin[...]
            arrived(first + 7, x0dir.at[y])
            arrived(first + 9, x0fin.at[y])
            part0 = s0[x, y] + x0dir[y] + x0fin[y]
            arrived(first + 13, y0r)
            part0 = part0 + y0r[...]
            gat[layer, chip] = attend(layer, g, part0, part1)

            first = ids(7)
            mine = gat.at[layer, chip]
            put(first + 0, mine, mine, to_ahead)
            put(first + 1, mine, mine, to_behind)
            put(first + 3, mine, mine, to_other_ahead)
            put(first + 4, mine, mine, to_other_behind)
            put(first + 2, mine, mine, to_other)
            yield
            places = ((0, y, behind), (3, other, behind), (1, y, ahead), (2, other, x), (4, other, ahead))
            places += ((5, y, far), (6, other, far))
            for number, py, px in places[:2]:
                block = gat.at[layer, py * 4 + px]
                arrived(first + number, block)
                put(first + (5 if number == 0 else 6), block, block, to_ahead)
            yield
            for number, py, px in places[2:]:
                arrived(first + number, gat.at[layer, py * 4 + px])
            if g == 0:
                rows = gat[layer].reshape(8 * count, 1024)
            else:
                blocks = gat[layer].astype(F32)
                rows = [jnp.concatenate([blocks[q, :count], blocks[q, count:]], axis=1) for q in range(8)]
                rows = jnp.concatenate(rows, axis=0).astype(BF16)
            ob[...] = dot(rows, wout[layer]).reshape(8, count, 2 * COLS)

            first = ids(7)
            d1r, d2r = refs["d1r"], refs["d2r"]
            for k in (3, 2, 1, 0):
                put(first + k, ob.at[chip_of(ring(-1 - k))], d1r.at[layer, k], partner)
            if layer == 0 and g == 1:
                begin_prompt(1)
                turn(1, 0)
            yield
            for k in (3, 2, 1):
                at = ring(k)
                block = ob.at[chip_of(at)]
                arrived(first + k, d1r.at[layer, k])
                block[...] = block[...] + d1r[layer, k]
                put(first + 3 + k, block, d2r.at[layer, k - 1], {"tensor": at})
            arrived(first + 0, d1r.at[layer, 0])
            stream = own[chip_of(z)] + ob[chip_of(z)] + d1r[layer, 0]
            if layer == 0 and g == 1:
                gathers[1].cross()
                gathers[1].along(0)
                turn(1, 1)
            yield
            for k in (1, 2, 3):
                arrived(first + 3 + k, d2r.at[layer, k - 1])
                stream = stream + d2r[layer, k - 1]
            tiles = [stream[:, 128 * t : 128 * t + 128] for t in range(5)]
            if layer == 0:
                own[chip_of(z)] = stream
                squares = jnp.sum(stream * stream, axis=1, keepdims=True)
                square1 = squares.astype(BF16).astype(F32)
                square2 = (squares - square1).astype(BF16).astype(F32)
                square3 = squares - square1 - square2
                line = iota((count, 128), 0)
                extra = jnp.zeros((count, 128), F32)
                for i, term in enumerate((square1, square2, square3)):
                    across = jnp.sum(jnp.where(diagonal, term, 0.0), axis=0, keepdims=True)
                    extra = jnp.where(line == i, across, extra)
                refs["sg"][z] = jnp.concatenate(tiles + [extra], axis=0).astype(BF16)
                yield from tensor_gather(refs["sg"], g)
                if g == 1:
                    gathers[1].last(0)
                    gathers[1].along(1)
                drain(g)
            else:
                fg, fs = refs["fg"], refs["fs"]
                for t in range(5):
                    fg[z, t] = tiles[t]
                crossing = ids(8)
                refs["crossing"] = crossing

                def hand_across(at):
                    put(crossing + at, fg.at[at, pl.ds(2 - 2 * core, 3)], fs.at[at], sibling)

                yield from tensor_gather(fg, g, hand_across)
                yield

    waiting = [chain(0), chain(1)]
    while waiting:
        for each in list(waiting):
            if next(each, "end") == "end":
                waiting.remove(each)

    def in_order(early, late):
        parts = []
        for j in range(NPR):
            parts += [early[4 * j : 4 * j + 4], late[2 * j : 2 * j + 2]]
        return jnp.concatenate(parts, axis=0)

    for at in range(8):
        for t in range(3):
            both = [buffers[g]["fg"][at, 2 * core + t] for g in range(2)]
            out_rows[my_rows(chip_of(at)), 128 * t : 128 * t + 128] = in_order(*both)
    for at in range(8):
        for g in range(2):
            arrived(buffers[g]["crossing"] + at, buffers[g]["fs"].at[at])
        theirs = pl.ds(pl.multiple_of(chip_of(at) * CHIP + (1 - core) * OWN, 8), OWN)
        for t in range(3):
            both = [buffers[g]["fs"][at, t] for g in range(2)]
            out_rows[theirs, 128 * t : 128 * t + 128] = in_order(*both)
    out_cols[...] = out_rows[...].T
    out_ref[...] = out_cols[pl.ds(pl.multiple_of(core * 64, 8), COLS), :]
    for each in range(3):
        drain(each)


NAMES = (
    "rows", "s0", "s1", "x0relay", "x0dir", "x0fin", "x1relay", "x1dir", "x1fin", "y1r", "y0r",
    "gat", "ob", "d1r", "d2r", "sg", "fg", "fs",
)


def group_scratch(count):
    vmem = pltpu.VMEM
    return [
        vmem((8, count, 2 * COLS), F32),
        vmem((4, 2, count, WIDE0), F32),
        vmem((2, 4, count, PART1), F32),
        *[vmem((LAYERS, 2, count, WIDE0), F32)] * 3,
        *[vmem((LAYERS, count, PART1), F32)] * 3,
        vmem((LAYERS, 4, count, PART1), F32),
        vmem((LAYERS, count, WIDE0), F32),
        vmem((LAYERS, 8, 16, 64 * count), BF16),
        vmem((8, count, 2 * COLS), F32),
        vmem((LAYERS, 4, count, 2 * COLS), F32),
        vmem((LAYERS, 3, count, 2 * COLS), F32),
        vmem((8, 6 * count, 128), BF16),
        vmem((8, 5, count, 128), F32),
        vmem((8, 3, count, 128), F32),
    ]


def on_device(hidden_in, prompt_len, cached_prompt_keys, cached_prompt_values, query_key_value_weight, w_out):
    keys = cached_prompt_keys.reshape(LAYERS, 128, HEAD)
    values = cached_prompt_values.reshape(LAYERS, 128, HEAD)
    half = np.power(ROPE_BASE, -2.0 * np.arange(64) / HEAD)
    freq = jnp.asarray(np.concatenate([half, half])[None, :], F32)
    vmem = pltpu.VMEM
    scratch = [
        vmem((2, COLS, ROWS), F32),
        vmem((ROWS, 2 * COLS), F32),
        vmem((LAYERS, 2, COLS, 1280), BF16),
        vmem((LAYERS, 2, COLS, 1024), BF16),
        vmem((LAYERS, 1024, 2 * COLS), BF16),
        vmem((LAYERS, 128, HEAD), BF16),
        vmem((LAYERS, 17, 2, 128, HEAD), BF16),
        vmem((2, 16, 128), F32),
        vmem((2, 16, 128), F32),
        vmem((2, 128, 128), jnp.int32),
        vmem((2, 128, 128), jnp.int32),
        vmem((16, HEAD), F32),
        vmem((ROWS, PAD), F32),
        vmem((PAD, ROWS), F32),
        *group_scratch(GROUPS[0]),
        *group_scratch(GROUPS[1]),
        pltpu.SemaphoreType.DMA((9,)),
        pltpu.SemaphoreType.DMA((COPIES,)),
        pltpu.SemaphoreType.DMA((COPIES,)),
    ]
    hbm = pl.BlockSpec(memory_space=pl.ANY)
    out = pl.pallas_call(
        kernel,
        out_shape=jax.ShapeDtypeStruct((COLS, ROWS), F32),
        in_specs=[
            pl.BlockSpec(memory_space=pltpu.SMEM),
            pl.BlockSpec(memory_space=pltpu.VMEM),
            hbm, hbm, hbm, hbm, hbm,
        ],
        out_specs=pl.BlockSpec(memory_space=pltpu.VMEM),
        scratch_shapes=scratch,
        compiler_params=pltpu.CompilerParams(
            collective_id=0, has_side_effects=True, vmem_limit_bytes=60 * 1024 * 1024
        ),
        name="two_layers",
    )(prompt_len, freq, hidden_in.T, keys, values, query_key_value_weight, w_out.transpose(0, 2, 1))
    return out.T


def solution(mesh):
    return jax.shard_map(
        on_device,
        mesh=mesh,
        in_specs=(
            P("prompt", "sample"),
            P("prompt"),
            P(None, ("prompt", "sample"), "tensor", None),
            P(None, ("prompt", "sample"), "tensor", None),
            P(None, "sample", "tensor"),
            P(None, "tensor", "sample"),
        ),
        out_specs=P("prompt", "sample"),
        check_vma=False,
    )
```
